32 devices in a mesh: section: 4 (over y, core), shard: 8 (over z, x).
Axes of the slice: x: 2, y: 2, z: 4, core: 2. Of those that a mesh axis runs over, the one named last changes fastest.
Arguments:
- activations: bfloat16 [4, 8, 32, 8192], P('section', None, None, 'shard'), may hold values from -6 to 6
- top_grad: bfloat16 [8, 32, 8192], P(None, None, 'shard'), may hold values from -6 to 6
- projection: bfloat16 [4, 8192, 8192], P('section', None, 'shard'), may hold values from -0.03125 to 0.03125
- basis_out: bfloat16 [4, 8192, 4096], P('section', None, 'shard'), may hold values from -0.0625 to 0.0625
- basis_in: bfloat16 [4, 8192, 4096], P('section', 'shard'), may hold values from -0.0625 to 0.0625
Outputs:
- eigenvalues: float32 [4, 4096, 4096], P('section', 'shard')
The draws below stay inside these ranges and needn't reach their ends.
All inputs are finite; a program needn't handle non-finite values.
Results may differ from the reference program's by a relative error of at most 0.007.
Values may be sent and summed in bfloat16 or wider, within the bound.
No kernel may reach another device: no remote copies, remote signals or barrier semaphores. Data moves between devices by JAX's collectives and lax.ppermute only.
A program may use at most 128 MiB of HBM per device.

```python
import jax
import jax.numpy as jnp
from jax import lax

D = 8192
EIG_G = 4096
EIG_A = 4096
SEQ = 32
MICRO = 8
SECTIONS = 4


def levels(stream_key, dims, shards, smallest, high):
    loudness, own = 1.0, jax.random.fold_in(stream_key, 6)
    for position, shards_of in shards:
        steps = jnp.exp(jax.random.uniform(jax.random.fold_in(own, position), (shards_of,), jnp.float32, smallest / len(shards), high / len(shards)))
        loudness = loudness * jnp.repeat(steps, dims[position] // shards_of).reshape([-1 if axis == position else 1 for axis in range(len(dims))])
    return loudness


def noise(stream_key, shape, deviation, bound, split=(), dtype=jnp.bfloat16):
    drawn = deviation * jax.random.normal(stream_key, shape, jnp.float32)
    if split:
        drawn = drawn * levels(stream_key, shape, split, -0.22, 0.18)
    return jnp.clip(drawn, -bound, bound).astype(dtype)


def setup_inputs(seed: int = 0) -> dict:
    keys = jax.random.split(jax.random.key(seed), 6)
    activations = noise(keys[0], (SECTIONS, MICRO, SEQ, D), 1.0, 6.0, ((0, 4), (3, 8)))
    top_grad = noise(keys[1], (MICRO, SEQ, D), 1.0, 6.0, ((2, 8),))
    projection = noise(keys[2], (SECTIONS, D, D), (4 * D) ** -0.5, 0.03125, ((0, 4), (2, 8)))
    basis_out = noise(keys[3], (SECTIONS, D, EIG_G), D ** -0.5, 0.0625, ((0, 4), (2, 8)))
    basis_in = noise(keys[4], (SECTIONS, D, EIG_A), D ** -0.5, 0.0625, ((0, 4), (1, 8)))
    return {"activations": activations, "top_grad": top_grad, "projection": projection, "basis_out": basis_out, "basis_in": basis_in}


def reference(activations, top_grad, projection, basis_out, basis_in):
    grads = top_grad
    results = []
    for section_num in range(SECTIONS - 1, -1, -1):
        rot_in = jnp.einsum('msd,de->mse', activations[section_num].astype(jnp.float32), basis_in[section_num].astype(jnp.float32)).astype(jnp.bfloat16)
        rot_out = jnp.einsum('msd,dg->msg', grads.astype(jnp.float32), basis_out[section_num].astype(jnp.float32)).astype(jnp.bfloat16)
        rotated = jnp.einsum('msg,mse->mge', rot_out.astype(jnp.float32), rot_in.astype(jnp.float32)) / jnp.sqrt(jnp.float32(SEQ))
        results.append(lax.optimization_barrier(jnp.sum(rotated * rotated, axis=0)) / MICRO)
        through = jnp.einsum('msd,de->mse', grads.astype(jnp.float32), projection[section_num].astype(jnp.float32))
        grads = (grads.astype(jnp.float32) + through).astype(jnp.bfloat16)
    return jnp.stack(results[::-1])
```

```python
import jax
import jax.numpy as jnp
from jax import lax
from jax.experimental import pallas as pl
from jax.experimental.pallas import tpu as pltpu
from jax.sharding import PartitionSpec as P

VMEM_LIMIT = 48 * 1024 * 1024


def gathered_dot(blocks, weights, base=None):
    parts, rows, depth = blocks.shape
    cols = weights.shape[1]
    group = max(1, min(parts, 1024 // depth))
    steps = parts // group

    def body(*refs):
        if base is None:
            blocks_ref, weights_ref, out_ref, total = refs
        else:
            blocks_ref, weights_ref, base_ref, out_ref, total = refs
        step = pl.program_id(0)

        @pl.when(step == 0)
        def _():
            if base is None:
                total[...] = jnp.zeros_like(total)
            else:
                total[...] = base_ref[...].astype(jnp.float32)

        for j in range(group):
            total[...] += jnp.dot(
                blocks_ref[j],
                weights_ref[j * depth : (j + 1) * depth, :],
                preferred_element_type=jnp.float32,
            )

        @pl.when(step == steps - 1)
        def _():
            out_ref[...] = total[...].astype(jnp.bfloat16)

    whole = pl.BlockSpec((rows, cols), lambda i: (0, 0))
    return pl.pallas_call(
        body,
        grid=(steps,),
        in_specs=[
            pl.BlockSpec((group, rows, depth), lambda i: (i, 0, 0)),
            pl.BlockSpec((group * depth, cols), lambda i: (i, 0)),
        ]
        + ([] if base is None else [whole]),
        out_specs=whole,
        out_shape=jax.ShapeDtypeStruct((rows, cols), jnp.bfloat16),
        scratch_shapes=[pltpu.VMEM((rows, cols), jnp.float32)],
        compiler_params=pltpu.CompilerParams(vmem_limit_bytes=VMEM_LIMIT),
        cost_estimate=pl.CostEstimate(
            flops=2 * parts * rows * depth * cols,
            bytes_accessed=2 * (parts * rows * depth + parts * depth * cols + rows * cols),
            transcendentals=0,
        ),
        name="gathered_dot",
    )(blocks, weights, *([] if base is None else [base]))


def mean_square(rot_out, rot_in, micro, seq):
    runs, rows, width = rot_in.shape
    eig_rows = rot_out.shape[1]

    def body(out_ref_in, in_ref, eig_ref):
        for m in range(micro):
            rows_of = slice(m * seq, (m + 1) * seq)
            product = lax.dot_general(
                out_ref_in[rows_of, :],
                in_ref[0, rows_of, :],
                (((0,), (0,)), ((), ())),
                preferred_element_type=jnp.float32,
            )
            square = product * product
            eig_ref[...] = square if m == 0 else eig_ref[...] + square
        eig_ref[...] *= 1.0 / (seq * micro)

    return pl.pallas_call(
        body,
        grid=(runs,),
        in_specs=[
            pl.BlockSpec((rows, eig_rows), lambda i: (0, 0)),
            pl.BlockSpec((1, rows, width), lambda i: (i, 0, 0)),
        ],
        out_specs=pl.BlockSpec((eig_rows, width), lambda i: (0, i)),
        out_shape=jax.ShapeDtypeStruct((eig_rows, runs * width), jnp.float32),
        compiler_params=pltpu.CompilerParams(vmem_limit_bytes=VMEM_LIMIT),
        cost_estimate=pl.CostEstimate(
            flops=2 * rows * eig_rows * runs * width * 8,
            bytes_accessed=4 * eig_rows * runs * width,
            transcendentals=0,
        ),
        name="mean_square",
    )(rot_out, rot_in)


def per_device(activations, top_grad, projection, basis_out, basis_in):
    sections = lax.axis_size("section")
    shards = lax.axis_size("shard")
    section = lax.axis_index("section")
    micro, seq, feat_loc = top_grad.shape
    rows = micro * seq
    eig_a = basis_in.shape[2]
    weights, out_cols = projection[0], basis_out[0]

    partial_rot = jnp.dot(
        activations[0].reshape(rows, feat_loc), basis_in[0], preferred_element_type=jnp.float32
    ).astype(jnp.bfloat16)
    partial_rot = partial_rot.reshape(rows, shards, eig_a // shards).transpose(1, 0, 2)
    own_rot = lax.psum_scatter(partial_rot, "shard", scatter_dimension=0, tiled=False)
    rot_in = lax.all_gather(own_rot, "shard", axis=0)

    current = top_grad.reshape(rows, feat_loc)
    rot_out = jnp.zeros((rows, out_cols.shape[1]), jnp.bfloat16)
    for step in range(sections):
        active = section == sections - 1 - step
        blocks = lax.all_gather(current, "shard", axis=0)
        if step < sections - 1:
            lower = gathered_dot(blocks, weights, current)
            route = [(sections - 1 - step, sections - 2 - step)]
            received = lax.ppermute(lower, "section", route)
        rot_out = lax.cond(
            active,
            lambda blocks, old: gathered_dot(blocks, out_cols),
            lambda blocks, old: old,
            blocks,
            rot_out,
        )
        if step < sections - 1:
            current = received
    return mean_square(rot_out, rot_in, micro, seq)[None]


def solution(mesh):
    return jax.shard_map(
        per_device,
        mesh=mesh,
        in_specs=(
            P("section", None, None, "shard"),
            P(None, None, "shard"),
            P("section", None, "shard"),
            P("section", None, "shard"),
            P("section", "shard", None),
        ),
        out_specs=P("section", "shard", None),
        check_vma=False,
    )
```

```python
import jax
import jax.numpy as jnp
from jax import lax
from jax.experimental import pallas as pl
from jax.experimental.pallas import tpu as pltpu
from jax.sharding import PartitionSpec as P

DOT_VMEM = 20 * 1024 * 1024
SQUARE_VMEM = 32 * 1024 * 1024


def blocks_dot(blocks, sources, weights, base, last):
    rows, depth = blocks[0].shape
    cols = weights.shape[1]
    count = len(blocks)
    halves = 2 if depth % 256 == 0 else 1
    tile = depth // halves

    def body(sources_ref, *refs):
        block_refs, rest = refs[:count], refs[count:]
        if base is None:
            weights_ref, out_ref, total = rest
        else:
            weights_ref, base_ref, out_ref, total = rest
        which, half = pl.program_id(0), pl.program_id(1)

        @pl.when((which == 0) & (half == 0))
        def _():
            if base is None:
                total[...] = jnp.zeros_like(total)
            else:
                total[...] = base_ref[...].astype(jnp.float32)

        for i in range(count):
            for j in range(halves):

                @pl.when((which == i) & (half == j))
                def _():
                    total[...] += jnp.dot(
                        block_refs[i][:, j * tile : (j + 1) * tile],
                        weights_ref[...],
                        preferred_element_type=jnp.float32,
                    )

        @pl.when((which == count - 1) & (half == halves - 1))
        def _():
            out_ref[...] = total[...].astype(out_ref.dtype)

    def whole(shape):
        return pl.BlockSpec(shape, lambda i, j, s: (0, 0))

    out_type = jnp.bfloat16 if last else jnp.float32
    return pl.pallas_call(
        body,
        grid_spec=pltpu.PrefetchScalarGridSpec(
            num_scalar_prefetch=1,
            grid=(count, halves),
            in_specs=[whole((rows, depth))] * count
            + [pl.BlockSpec((tile, cols), lambda i, j, s: (s[i] * halves + j, 0))]
            + ([] if base is None else [whole((rows, cols))]),
            out_specs=whole((rows, cols)),
            scratch_shapes=[pltpu.VMEM((rows, cols), jnp.float32)],
        ),
        out_shape=jax.ShapeDtypeStruct((rows, cols), out_type),
        compiler_params=pltpu.CompilerParams(vmem_limit_bytes=DOT_VMEM),
        cost_estimate=pl.CostEstimate(
            flops=2 * count * rows * depth * cols,
            bytes_accessed=2 * count * (rows + cols) * depth,
            transcendentals=0,
        ),
        name="blocks_dot",
    )(jnp.stack(sources).astype(jnp.int32), *blocks, weights, *([] if base is None else [base]))


def gather_blocks(own, section, shards, inner):
    def swapped(block, flip):
        here = [section * shards + i for i in range(shards)]
        there = [section * shards + (i ^ flip) for i in range(shards)]
        return lax.ppermute(block, ("section", "shard"), list(zip(here, there)))

    got = {(0, 0): own}
    for dz in range(1, shards // inner):
        got[dz, 0] = swapped(own, dz * inner)
    for dz in range(shards // inner):
        for dx in range(1, inner):
            got[dz, dx] = swapped(got[dz, 0], dx)
    return got


def mean_square(rot_out, rot_in, micro, seq):
    runs, rows, width = rot_in.shape
    eig_rows = rot_out.shape[1]

    def body(out_ref_in, in_ref, eig_ref):
        for m in range(micro):
            rows_of = slice(m * seq, (m + 1) * seq)
            product = lax.dot_general(
                out_ref_in[rows_of, :],
                in_ref[0, rows_of, :],
                (((0,), (0,)), ((), ())),
                preferred_element_type=jnp.float32,
            )
            square = product * product
            eig_ref[...] = square if m == 0 else eig_ref[...] + square
        eig_ref[...] *= 1.0 / (seq * micro)

    return pl.pallas_call(
        body,
        grid=(runs,),
        in_specs=[
            pl.BlockSpec((rows, eig_rows), lambda i: (0, 0)),
            pl.BlockSpec((1, rows, width), lambda i: (i, 0, 0)),
        ],
        out_specs=pl.BlockSpec((eig_rows, width), lambda i: (0, i)),
        out_shape=jax.ShapeDtypeStruct((eig_rows, runs * width), jnp.float32),
        compiler_params=pltpu.CompilerParams(vmem_limit_bytes=SQUARE_VMEM),
        cost_estimate=pl.CostEstimate(
            flops=2 * rows * eig_rows * runs * width * 8,
            bytes_accessed=4 * eig_rows * runs * width,
            transcendentals=0,
        ),
        name="mean_square",
    )(rot_out, rot_in)


def per_device(activations, top_grad, projection, basis_out, basis_in):
    sections = lax.axis_size("section")
    shards = lax.axis_size("shard")
    section = lax.axis_index("section")
    micro, seq, feat_loc = top_grad.shape
    rows = micro * seq
    eig_a = basis_in.shape[2]
    weights, out_cols = projection[0], basis_out[0]

    partial_rot = jnp.dot(
        activations[0].reshape(rows, feat_loc), basis_in[0], preferred_element_type=jnp.float32
    ).astype(jnp.bfloat16)
    partial_rot = partial_rot.reshape(rows, shards, eig_a // shards).transpose(1, 0, 2)
    own_rot = lax.psum_scatter(partial_rot, "shard", scatter_dimension=0, tiled=False)
    rot_in = lax.all_gather(own_rot, "shard", axis=0)

    inner = 1
    while 2 * (2 * inner) ** 2 <= shards:
        inner *= 2
    shard = lax.axis_index("shard")
    current = top_grad.reshape(rows, feat_loc)
    rot_out = None
    for step in range(sections):
        turn = sections - 1 - step
        blocks = gather_blocks(current, turn, shards, inner)
        source = {(dz, dx): shard ^ (dz * inner + dx) for dz, dx in blocks}
        groups = [[(dz, dx) for dx in range(inner)] for dz in range(shards // inner)]
        final = turn == 0
        total = None if final else current
        for n, group in enumerate(groups):
            total = blocks_dot(
                [blocks[g] for g in group],
                [source[g] for g in group],
                out_cols if final else weights,
                total,
                n == len(groups) - 1,
            )
        if final:
            rot_out = total if rot_out is None else jnp.where(section == 0, total, rot_out)
            break
        received = lax.ppermute(total, "section", [(turn, turn - 1)])
        flat = list(blocks.values())
        rot_out = lax.cond(
            section == turn,
            lambda *a: blocks_dot(a[1:], list(source.values()), out_cols, None, True),
            lambda *a: a[0],
            jnp.zeros((rows, out_cols.shape[1]), jnp.bfloat16) if rot_out is None else rot_out,
            *flat,
        )
        current = received
    return mean_square(rot_out, rot_in, micro, seq)[None]


def solution(mesh):
    return jax.shard_map(
        per_device,
        mesh=mesh,
        in_specs=(
            P("section", None, None, "shard"),
            P(None, None, "shard"),
            P("section", None, "shard"),
            P("section", None, "shard"),
            P("section", "shard", None),
        ),
        out_specs=P("section", "shard", None),
        check_vma=False,
    )
```

```python
import jax
import jax.numpy as jnp
from jax import lax
from jax.experimental import pallas as pl
from jax.experimental.pallas import tpu as pltpu
from jax.sharding import PartitionSpec as P

DOT_VMEM = 50 * 1024 * 1024
SQUARE_VMEM = 40 * 1024 * 1024


def tile_dot(blocks, weights, picks, bases, out_type, cols, by_rows):
    rows, depth = blocks[0].shape
    count = len(blocks)
    width = 256 if cols % 256 == 0 else cols
    tiles = cols // width

    def body(picks_ref, *refs):
        total = None
        for block_ref, weight_ref in zip(refs[:count], refs[count : 2 * count]):
            part = jnp.dot(block_ref[...], weight_ref[...], preferred_element_type=jnp.float32)
            total = part if total is None else total + part
        for base_ref in refs[2 * count : -1]:
            total = total + base_ref[...].astype(jnp.float32)
        refs[-1][...] = total.astype(out_type)

    def weight_spec(i):
        if by_rows:
            return pl.BlockSpec((depth, width), lambda j, picked: (picked[i], j))
        return pl.BlockSpec((depth, width), lambda j, picked: (0, picked[i] * tiles + j))

    tile = pl.BlockSpec((rows, width), lambda j, picked: (0, j))
    whole = pl.BlockSpec((rows, depth), lambda j, picked: (0, 0))
    return pl.pallas_call(
        body,
        grid_spec=pltpu.PrefetchScalarGridSpec(
            num_scalar_prefetch=1,
            grid=(tiles,),
            in_specs=[whole] * count + [weight_spec(i) for i in range(count)] + [tile] * len(bases),
            out_specs=tile,
        ),
        out_shape=jax.ShapeDtypeStruct((rows, cols), out_type),
        compiler_params=pltpu.CompilerParams(vmem_limit_bytes=DOT_VMEM),
        cost_estimate=pl.CostEstimate(
            flops=2 * count * rows * depth * cols,
            bytes_accessed=2 * count * (rows + cols) * depth,
            transcendentals=0,
        ),
        name="tile_dot",
    )(jnp.stack(picks).astype(jnp.int32), *blocks, *[weights] * count, *bases)


def dot_if(active, blocks, weights, picks, bases, out_type, cols, by_rows):
    count = len(blocks)

    def run(*args):
        blocks, bases = args[:count], args[count:]
        return tile_dot(blocks, weights, picks, bases, out_type, cols, by_rows)

    def skip(*args):
        return jnp.zeros((args[0].shape[0], cols), out_type)

    return lax.cond(active, run, skip, *blocks, *bases)


def mean_square(rot_out, blocks, picks, micro, seq):
    count = len(blocks)
    rows, width = blocks[0].shape
    eig_rows = rot_out.shape[1]

    def body(picks_ref, out_ref_in, *refs):
        block_refs, eig_ref, block = refs[:count], refs[count], refs[count + 1]
        for i in range(count):

            @pl.when(pl.program_id(0) == i)
            def _():
                block[...] = block_refs[i][...]

        for m in range(micro):
            rows_of = slice(m * seq, (m + 1) * seq)
            product = lax.dot_general(
                out_ref_in[rows_of, :],
                block[rows_of, :],
                (((0,), (0,)), ((), ())),
                preferred_element_type=jnp.float32,
            )
            square = product * product
            eig_ref[...] = square if m == 0 else eig_ref[...] + square
        eig_ref[...] *= 1.0 / (seq * micro)

    return pl.pallas_call(
        body,
        grid_spec=pltpu.PrefetchScalarGridSpec(
            num_scalar_prefetch=1,
            grid=(count,),
            in_specs=[pl.BlockSpec((rows, eig_rows), lambda i, picked: (0, 0))]
            + [pl.BlockSpec((rows, width), lambda i, picked: (0, 0))] * count,
            out_specs=pl.BlockSpec((eig_rows, width), lambda i, picked: (0, picked[i])),
            scratch_shapes=[pltpu.VMEM((rows, width), jnp.bfloat16)],
        ),
        out_shape=jax.ShapeDtypeStruct((eig_rows, count * width), jnp.float32),
        compiler_params=pltpu.CompilerParams(vmem_limit_bytes=SQUARE_VMEM),
        cost_estimate=pl.CostEstimate(
            flops=16 * rows * eig_rows * count * width,
            bytes_accessed=4 * eig_rows * count * width,
            transcendentals=0,
        ),
        name="mean_square",
    )(jnp.stack(picks).astype(jnp.int32), rot_out, *blocks)


def per_device(activations, top_grad, projection, basis_out, basis_in):
    sections = lax.axis_size("section")
    shards = lax.axis_size("shard")
    section, shard = lax.axis_index("section"), lax.axis_index("shard")
    micro, seq, feat_loc = top_grad.shape
    rows = micro * seq
    width = basis_in.shape[2] // shards
    weights, out_cols, in_cols = projection[0], basis_out[0], basis_in[0]
    inputs = activations[0].reshape(rows, feat_loc)
    top = top_grad.reshape(rows, feat_loc)

    inner = 1
    while 2 * (2 * inner) ** 2 <= shards:
        inner *= 2
    outer = shards // inner
    steps = [(dz, dx) for dz in range(outer) for dx in range(inner)]
    picks = {(dz, dx): shard ^ (dz * inner + dx) for dz, dx in steps}

    def moved(block, flip, pairs):
        route = [(a * shards + i, b * shards + (i ^ flip)) for a, b in pairs for i in range(shards)]
        return lax.ppermute(block, ("section", "shard"), route)

    def spread(block, pairs):
        stays = all(a == b for a, b in pairs)
        sent = {0: block if stays else moved(block, 0, pairs)}
        dz = 1
        while dz < outer:
            sent[dz] = moved(block, dz * inner, pairs)
            dz *= 2
        return sent

    def gather(sent, among):
        pairs = [(a, a) for a in among]
        got = {}
        for dz in range(outer):
            low = dz & -dz
            if low == dz:
                got[dz, 0] = sent[dz]
            else:
                got[dz, 0] = moved(got[dz ^ low, 0], low * inner, pairs)
            for dx in range(1, inner):
                low_x = dx & -dx
                got[dz, dx] = moved(got[dz, dx ^ low_x], low_x, pairs)
        return got

    groups = [[(dz, dx) for dx in range(inner)] for dz in range(outer)]
    if inner > 1:
        groups = groups[:-1] + [groups[-1][:-1], groups[-1][-1:]]

    def chain(sent, turns, rot_out):
        for turn in turns:
            mine = section == turn
            got = gather(sent, [turn])
            got[0, 0], rot_out = lax.optimization_barrier((got[0, 0], rot_out))
            final = turn == 0
            matrix = out_cols if final else weights
            bases = [] if final else [got[0, 0]]
            for n, group in enumerate(groups):
                total = dot_if(
                    mine,
                    [got[g] for g in group],
                    matrix,
                    [picks[g] for g in group],
                    bases,
                    jnp.bfloat16 if n == len(groups) - 1 else jnp.float32,
                    matrix.shape[1],
                    True,
                )
                bases = [total]
            if final:
                return jnp.where(mine, total, rot_out)
            sent = spread(total, [(turn, turn - 1)])
            rot_out = lax.cond(
                mine,
                lambda old, *blocks: tile_dot(
                    blocks,
                    out_cols,
                    [picks[g] for g in steps],
                    [],
                    jnp.bfloat16,
                    out_cols.shape[1],
                    True,
                ),
                lambda old, *blocks: old,
                rot_out,
                *[got[g] for g in steps],
            )
        return sent, rot_out

    def rotate_in(inputs, among):
        pairs = [(a, a) for a in among]
        mine = (section >= min(among)) & (section <= max(among))

        def product(dz, dx, bases):
            return dot_if(
                mine, [inputs], in_cols, [picks[dz, dx]], bases, jnp.bfloat16, width, False
            )

        crossed = {
            dz: [moved(product(dz, dx, []), dx, pairs) for dx in range(1, inner)]
            for dz in [*range(1, outer), 0]
        }
        arrived = [
            moved(product(dz, 0, crossed[dz]), dz * inner, pairs) for dz in range(1, outer)
        ]
        own = product(0, 0, crossed[0] + arrived)
        got = gather(spread(own, pairs), among)
        return [got[g] for g in steps]

    half = sections // 2
    upper = list(range(sections - 1, half - 1, -1))
    lower = list(range(half - 1, -1, -1))
    sent = spread(top, [(upper[0], upper[0])])
    rot_out = jnp.zeros((rows, out_cols.shape[1]), jnp.bfloat16)
    sent, rot_out = chain(sent, upper, rot_out)
    low_rot_in = rotate_in(inputs, lower)
    sent, low_rot_in, inputs = lax.optimization_barrier((sent, low_rot_in, inputs))
    rot_out = chain(sent, lower, rot_out)
    high_rot_in = rotate_in(inputs, upper)
    eigenvalues = lax.cond(
        section >= half,
        lambda rot_out, low, high: mean_square(rot_out, high, [picks[g] for g in steps], micro, seq),
        lambda rot_out, low, high: mean_square(rot_out, low, [picks[g] for g in steps], micro, seq),
        rot_out,
        low_rot_in,
        high_rot_in,
    )
    return eigenvalues[None]


def solution(mesh):
    return jax.shard_map(
        per_device,
        mesh=mesh,
        in_specs=(
            P("section", None, None, "shard"),
            P(None, None, "shard"),
            P("section", None, "shard"),
            P("section", None, "shard"),
            P("section", "shard", None),
        ),
        out_specs=P("section", "shard", None),
        check_vma=False,
    )
```

```python
import jax
import jax.numpy as jnp
from jax import lax
from jax.experimental import pallas as pl
from jax.experimental.pallas import tpu as pltpu
from jax.sharding import PartitionSpec as P

DOT_VMEM = 10 * 1024 * 1024
VMEM = pl.BlockSpec(memory_space=pltpu.VMEM)
SMEM = pl.BlockSpec(memory_space=pltpu.SMEM)
ANY = pl.BlockSpec(memory_space=pl.ANY)


def scalars(*values):
    return jnp.stack([jnp.asarray(v).astype(jnp.int32) for v in values])


def params():
    return pltpu.CompilerParams(vmem_limit_bytes=DOT_VMEM)


def cost(flops, moved):
    return pl.CostEstimate(flops=flops, bytes_accessed=moved, transcendentals=0)


def resident(active, weights, picks, by_rows):
    count = len(picks)
    shape = list(weights.shape)
    shape[0 if by_rows else 1] //= count
    run = shape[0 if by_rows else 1]

    def body(at, weights_ref, out_ref, sems):
        def copy(i):
            part = pl.ds(pl.multiple_of(at[1 + i] * run, run), run)
            source = weights_ref.at[part, :] if by_rows else weights_ref.at[:, part]
            return pltpu.make_async_copy(source, out_ref.at[i], sems.at[i])

        @pl.when(at[0] == 1)
        def _():
            for i in range(count):
                copy(i).start()
            for i in range(count):
                copy(i).wait()

    return pl.pallas_call(
        body,
        in_specs=[SMEM, ANY],
        out_specs=VMEM,
        out_shape=jax.ShapeDtypeStruct((count, *shape), weights.dtype),
        scratch_shapes=[pltpu.SemaphoreType.DMA((count,))],
        compiler_params=params(),
        cost_estimate=cost(0, 2 * weights.size),
        name="resident",
    )(scalars(active, *picks), weights)


def block_dot(active, blocks, weights, wanted, base, out_type):
    _, rows, depth = blocks[0].shape
    cols = weights.shape[2]
    width = 256 if cols % 256 == 0 else cols
    count = len(blocks)

    def body(active_ref, *refs):
        block_refs, weights_ref = refs[:count], refs[count]
        base_ref, out_ref = (None if base is None else refs[count + 1]), refs[-1]

        @pl.when(active_ref[0] == 1)
        def _():
            def tile(j, _):
                here = pl.ds(pl.multiple_of(j * width, width), width)
                total = None if base is None else base_ref[:, here].astype(jnp.float32)
                for a, i, w in wanted:
                    part = jnp.dot(
                        block_refs[a][i],
                        weights_ref[w, :, here],
                        preferred_element_type=jnp.float32,
                    )
                    total = part if total is None else total + part
                out_ref[:, here] = total.astype(out_type)
                return 0

            lax.fori_loop(0, cols // width, tile, 0)

    return pl.pallas_call(
        body,
        in_specs=[SMEM] + [VMEM] * (count + 1 + (base is not None)),
        out_specs=VMEM,
        out_shape=jax.ShapeDtypeStruct((rows, cols), out_type),
        compiler_params=params(),
        cost_estimate=cost(2 * len(wanted) * rows * depth * cols, rows * cols),
        name="block_dot",
    )(scalars(active), *blocks, weights, *([] if base is None else [base]))


def rotate_more(active, old, blocks, weights, wanted):
    _, rows, depth = blocks[0].shape
    cols = weights.shape[2]
    width = 256 if cols % 256 == 0 else cols
    count = len(blocks)

    def body(active_ref, *refs):
        block_refs, weights_ref, old_ref, out_ref = refs[:count], refs[count], refs[-2], refs[-1]

        @pl.when(active_ref[0] == 0)
        def _():
            out_ref[...] = old_ref[...]

        @pl.when(active_ref[0] == 1)
        def _():
            def tile(j, _):
                here = pl.ds(pl.multiple_of(j * width, width), width)
                total = None
                for a, i, w in wanted:
                    part = jnp.dot(
                        block_refs[a][i],
                        weights_ref[w, :, here],
                        preferred_element_type=jnp.float32,
                    )
                    total = part if total is None else total + part
                out_ref[:, here] = total.astype(out_ref.dtype)
                return 0

            lax.fori_loop(0, cols // width, tile, 0)

    return pl.pallas_call(
        body,
        in_specs=[SMEM] + [VMEM] * (count + 2),
        out_specs=VMEM,
        out_shape=jax.ShapeDtypeStruct((rows, cols), old.dtype),
        compiler_params=params(),
        cost_estimate=cost(2 * len(wanted) * rows * depth * cols, rows * cols),
        name="rotate_more",
    )(scalars(active), *blocks, weights, old)


def partials(active, inputs, weights, wanted, arrived, out_types, joined):
    rows, depth = inputs.shape
    width = weights.shape[2]
    count = len(arrived)

    def body(active_ref, inputs_ref, weights_ref, *refs):
        arrived_refs, out_refs = refs[:count], refs[count:]

        @pl.when(active_ref[0] == 1)
        def _():
            for n, (w, adds) in enumerate(wanted):
                total = jnp.dot(
                    inputs_ref[...], weights_ref[w], preferred_element_type=jnp.float32
                )
                for a, i in adds:
                    total = total + arrived_refs[a][i].astype(jnp.float32)
                out_ref = out_refs[0] if joined else out_refs[n]
                out_ref[n if joined else 0] = total.astype(out_ref.dtype)

    if joined:
        shapes = [jax.ShapeDtypeStruct((len(wanted), rows, width), out_types[0])]
    else:
        shapes = [jax.ShapeDtypeStruct((1, rows, width), t) for t in out_types]
    return pl.pallas_call(
        body,
        in_specs=[SMEM] + [VMEM] * (2 + count),
        out_specs=[VMEM] * len(shapes),
        out_shape=shapes,
        compiler_params=params(),
        cost_estimate=cost(2 * len(wanted) * rows * depth * width, rows * width),
        name="partials",
    )(scalars(active), inputs, weights, *arrived)


def mean_square(upper, rot_out, low, high, runs, picks, micro, seq):
    _, rows, width = low[0].shape
    eig_rows = rot_out.shape[1]
    count = len(runs)
    tall = 128 if eig_rows % 128 == 0 else eig_rows
    wide = 256 if width % 256 == 0 else width
    across = width // wide

    def body(at, rot_ref, *refs):
        low_refs, high_refs = refs[: len(low)], refs[len(low) : 2 * len(low)]
        eig_ref, turned, block, result, sems = refs[2 * len(low) :]
        for m in range(micro):
            turned[m] = rot_ref[m * seq : (m + 1) * seq, :].T

        def copy(n):
            columns = pl.ds(pl.multiple_of(at[1 + n] * width, width), width)
            return pltpu.make_async_copy(result.at[n % 2], eig_ref.at[:, columns], sems.at[n % 2])

        for n, (a, i) in enumerate(runs):

            @pl.when(at[0] == 1)
            def _():
                block[...] = high_refs[a][i]

            @pl.when(at[0] == 0)
            def _():
                block[...] = low_refs[a][i]

            if n >= 2:
                copy(n - 2).wait()

            def tile(t, _):
                down = pl.ds(pl.multiple_of((t // across) * tall, tall), tall)
                here = pl.ds(pl.multiple_of((t % across) * wide, wide), wide)
                total = None
                for m in range(micro):
                    product = jnp.dot(
                        turned[m, down, :],
                        block[m * seq : (m + 1) * seq, here],
                        preferred_element_type=jnp.float32,
                    )
                    square = product * product
                    total = square if total is None else total + square
                result[n % 2, down, here] = total * (1.0 / (seq * micro))
                return 0

            lax.fori_loop(0, (eig_rows // tall) * across, tile, 0)
            copy(n).start()
        for n in range(max(0, count - 2), count):
            copy(n).wait()

    return pl.pallas_call(
        body,
        in_specs=[SMEM] + [VMEM] * (1 + 2 * len(low)),
        out_specs=ANY,
        out_shape=jax.ShapeDtypeStruct((eig_rows, count * width), jnp.float32),
        scratch_shapes=[
            pltpu.VMEM((micro, eig_rows, seq), rot_out.dtype),
            pltpu.VMEM((rows, width), rot_out.dtype),
            pltpu.VMEM((2, eig_rows, width), jnp.float32),
            pltpu.SemaphoreType.DMA((2,)),
        ],
        compiler_params=params(),
        cost_estimate=cost(16 * rows * eig_rows * count * width, 4 * eig_rows * count * width),
        name="mean_square",
    )(scalars(upper, *picks), rot_out, *low, *high)


def per_device(activations, top_grad, projection, basis_out, basis_in):
    sections = lax.axis_size("section")
    shards = lax.axis_size("shard")
    section, shard = lax.axis_index("section"), lax.axis_index("shard")
    micro, seq, feat_loc = top_grad.shape
    rows = micro * seq
    inputs = activations[0].reshape(rows, feat_loc)
    top = top_grad.reshape(1, rows, feat_loc)
    half = sections // 2

    inner = 1
    while 2 * (2 * inner) ** 2 <= shards:
        inner *= 2
    outer = shards // inner
    picks = [shard ^ part for part in range(shards)]

    def moved(block, flip, pairs):
        route = [(a * shards + i, b * shards + (i ^ flip)) for a, b in pairs for i in range(shards)]
        return lax.ppermute(block, ("section", "shard"), route)

    def spread(block, pairs):
        stays = all(a == b for a, b in pairs)
        sent = {0: block if stays else moved(block, 0, pairs)}
        dz = 1
        while dz < outer:
            sent[dz] = moved(block, dz * inner, pairs)
            dz *= 2
        return sent

    def along_outer(sent, pairs):
        got = dict(sent)
        for dz in range(outer):
            low = dz & -dz
            if dz not in got:
                got[dz] = moved(got[dz ^ low], low * inner, pairs)
        return got

    def along_inner(blocks, pairs):
        return {dx: moved(blocks, dx, pairs) for dx in range(1, inner)}

    def chain(sent, turns, rot_out, weights, out_cols):
        for turn in turns:
            mine = section == turn
            pairs = [(turn, turn)]
            matrix = out_cols if turn == 0 else weights
            sent[0], rot_out = lax.optimization_barrier((sent[0], rot_out))
            total = None if turn == 0 else sent[0].reshape(rows, feat_loc)
            every = []
            batches = [[0]] + ([list(range(1, outer - 1))] if outer > 2 else []) + [[outer - 1]]
            got = along_outer(sent, pairs)
            for n, batch in enumerate(batches):
                near = [got[dz] for dz in batch]
                if n == len(batches) - 1 and total is not None:
                    near[0], total = lax.optimization_barrier((near[0], total))
                joined = near[0] if len(near) == 1 else jnp.concatenate(near)
                far = along_inner(joined, pairs)
                own = [(joined, [(i, dz * inner) for i, dz in enumerate(batch)])]
                other = [(far[dx], [(i, dz * inner + dx) for i, dz in enumerate(batch)]) for dx in far]
                every += own + other
                last = n == len(batches) - 1
                for part, group in enumerate([own, other] if last or n else [own + other]):
                    if not group:
                        continue
                    final = last and (part == 1 or not other)
                    total = block_dot(
                        mine,
                        [a for a, _ in group],
                        matrix,
                        [(k, i, w) for k, (_, uses) in enumerate(group) for i, w in uses],
                        total,
                        jnp.bfloat16 if final else jnp.float32,
                    )
            if turn == 0:
                return jnp.where(mine, total, rot_out)
            sent = spread(total.reshape(1, rows, feat_loc), [(turn, turn - 1)])
            rot_out = rotate_more(
                mine,
                rot_out,
                [a for a, _ in every],
                out_cols,
                [(k, i, w) for k, (_, uses) in enumerate(every) for i, w in uses],
            )
        return sent, rot_out

    def rotate_in(inputs, among):
        pairs = [(a, a) for a in among]
        mine = (section >= min(among)) & (section <= max(among))
        in_cols = resident(mine, basis_in[0], picks, False)
        first = list(range(1, 1 + outer // 2))
        second = list(range(1 + outer // 2, outer)) + [0]
        crossed = {}
        for batch in (first, second):
            crossed[batch[0]] = []
            for dx in range(1, inner):
                (sent,) = partials(
                    mine,
                    inputs,
                    in_cols,
                    [(dz * inner + dx, []) for dz in batch],
                    [],
                    [jnp.bfloat16],
                    True,
                )
                crossed[batch[0]].append(moved(sent, dx, pairs))
        arrived = []
        for batch in (first, second):
            sums = partials(
                mine,
                inputs,
                in_cols,
                [
                    (dz * inner, [(a, n) for a in range(inner - 1)])
                    for n, dz in enumerate(batch)
                ],
                crossed[batch[0]],
                [jnp.bfloat16 if dz else jnp.float32 for dz in batch],
                False,
            )
            arrived += [moved(s, dz * inner, pairs) for s, dz in zip(sums, batch) if dz]
        own = sums[-1]
        for other in arrived:
            own = own + other.astype(jnp.float32)
        got = along_outer(spread(own.astype(jnp.bfloat16), pairs), pairs)
        arrays, runs = [], {}
        for batch in (list(range(outer // 2)), list(range(outer // 2, outer))):
            near = jnp.concatenate([got[dz] for dz in batch])
            for dx, blocks in {0: near, **along_inner(near, pairs)}.items():
                for i, dz in enumerate(batch):
                    runs[dz * inner + dx] = (len(arrays), i)
                arrays.append(blocks)
        return arrays, [runs[n] for n in range(shards)]

    upper = list(range(sections - 1, half - 1, -1))
    lower = list(range(half - 1, -1, -1))
    weights = resident(True, projection[0], picks, True)
    out_cols = resident(True, basis_out[0], picks, True)
    rot_out = jnp.zeros((rows, basis_out.shape[2]), jnp.bfloat16)

    sent = spread(top, [(upper[0], upper[0])])
    sent, rot_out = chain(sent, upper, rot_out, weights, out_cols)
    low, runs = rotate_in(inputs, lower)
    sent, low, inputs = lax.optimization_barrier((sent, low, inputs))
    rot_out = chain(sent, lower, rot_out, weights, out_cols)
    high, runs = rotate_in(inputs, upper)
    return mean_square(section >= half, rot_out, low, high, runs, picks, micro, seq)[None]


def solution(mesh):
    return jax.shard_map(
        per_device,
        mesh=mesh,
        in_specs=(
            P("section", None, None, "shard"),
            P(None, None, "shard"),
            P("section", None, "shard"),
            P("section", None, "shard"),
            P("section", "shard", None),
        ),
        out_specs=P("section", "shard", None),
        check_vma=False,
    )
```

```python
import jax
import jax.numpy as jnp
from jax import lax
from jax.experimental import pallas as pl
from jax.experimental.pallas import tpu as pltpu
from jax.sharding import PartitionSpec as P

DOT_VMEM = 24 * 1024 * 1024
VMEM = pl.BlockSpec(memory_space=pltpu.VMEM)
SMEM = pl.BlockSpec(memory_space=pltpu.SMEM)
HBM = pl.BlockSpec(memory_space=pltpu.HBM)


def scalars(*values):
    return jnp.stack([jnp.asarray(v).astype(jnp.int32) for v in values])


def params():
    return pltpu.CompilerParams(vmem_limit_bytes=DOT_VMEM)


def cost(flops, moved):
    return pl.CostEstimate(flops=flops, bytes_accessed=moved, transcendentals=0)


def in_hbm(array):
    return pltpu.with_memory_space_constraint(array, pltpu.HBM)


def run_of(ref, axis, at, length):
    part = pl.ds(pl.multiple_of(at * length, length), length)
    return ref.at[part, :] if axis == 0 else ref.at[:, part]


def resident(weights, picks):
    count = len(picks)
    depth, cols = weights.shape[0] // count, weights.shape[1]

    def body(at, weights_ref, out_ref, sems):
        def copy(i):
            return pltpu.make_async_copy(
                run_of(weights_ref, 0, at[i], depth), out_ref.at[i], sems.at[i]
            )

        for i in range(count):
            copy(i).start()
        for i in range(count):
            copy(i).wait()

    return pl.pallas_call(
        body,
        in_specs=[SMEM, HBM],
        out_specs=VMEM,
        out_shape=jax.ShapeDtypeStruct((count, depth, cols), weights.dtype),
        scratch_shapes=[pltpu.SemaphoreType.DMA((count,))],
        compiler_params=params(),
        cost_estimate=cost(0, 2 * weights.size),
        name="resident",
    )(scalars(*picks), in_hbm(weights))


def block_dot(active, blocks, weights, wanted, base, out_type):
    rows, depth = blocks[0].shape
    cols = weights.shape[2]
    width = 256 if cols % 256 == 0 else cols
    count = len(blocks)

    def body(active_ref, weights_ref, base_ref, *refs):
        @pl.when(active_ref[0] == 1)
        def _():
            def tile(j, _):
                here = pl.ds(pl.multiple_of(j * width, width), width)
                total = base_ref[:, here].astype(jnp.float32)
                for block_ref, w in zip(refs[:count], wanted):
                    total += jnp.dot(
                        block_ref[...], weights_ref[w, :, here], preferred_element_type=jnp.float32
                    )
                refs[count][:, here] = total.astype(out_type)
                return 0

            lax.fori_loop(0, cols // width, tile, 0)

    return pl.pallas_call(
        body,
        in_specs=[SMEM] + [VMEM] * (count + 2),
        out_specs=VMEM,
        out_shape=jax.ShapeDtypeStruct((rows, cols), out_type),
        compiler_params=params(),
        cost_estimate=cost(2 * count * rows * depth * cols, rows * cols),
        name="block_dot",
    )(scalars(active), weights, base, *blocks)


def stream_dot(active, blocks, weights, picks, base, out_type, kept):
    rows, depth = blocks[0].shape
    cols = weights.shape[1]
    count = len(blocks)

    def body(at, weights_ref, base_ref, *refs):
        block_refs, (out_ref, runs, sems) = refs[:count], refs[count:]

        def copy(k):
            return pltpu.make_async_copy(
                run_of(weights_ref, 0, at[1 + k], depth), runs.at[k], sems.at[k]
            )

        @pl.when(at[0] == 1)
        def _():
            for k in range(count):
                copy(k).start()
            total = None if kept else base_ref[...]
            for k in range(count):
                copy(k).wait()
                part = jnp.dot(block_refs[k][...], runs[k], preferred_element_type=jnp.float32)
                total = part if total is None else total + part
            out_ref[...] = total.astype(out_type)

    return pl.pallas_call(
        body,
        in_specs=[SMEM, HBM] + [VMEM] * (count + 1),
        out_specs=VMEM,
        out_shape=jax.ShapeDtypeStruct((rows, cols), out_type),
        scratch_shapes=[
            pltpu.VMEM((count, depth, cols), weights.dtype),
            pltpu.SemaphoreType.DMA((count,)),
        ],
        input_output_aliases={2: 0} if kept else {},
        compiler_params=params(),
        cost_estimate=cost(2 * count * rows * depth * cols, 2 * count * depth * cols),
        name="stream_dot",
    )(scalars(active, *picks), in_hbm(weights), base, *blocks)


def partials(active, inputs, weights, picks, inner):
    rows, depth = inputs.shape
    count = len(picks)
    width = weights.shape[1] // count

    def body(at, weights_ref, inputs_ref, *refs):
        out_refs, (runs, sems) = refs[:inner], refs[inner:]
        order = [n for dx in [*range(1, inner), 0] for n in range(dx, count, inner)]

        def copy(n):
            return pltpu.make_async_copy(
                run_of(weights_ref, 1, at[1 + n], width), runs.at[n], sems.at[n]
            )

        @pl.when(at[0] == 1)
        def _():
            for n in order:
                copy(n).start()
            for n in order:
                copy(n).wait()
                total = jnp.dot(inputs_ref[...], runs[n], preferred_element_type=jnp.float32)
                out_ref = out_refs[n % inner]
                out_ref[n // inner] = total.astype(out_ref.dtype)

    return pl.pallas_call(
        body,
        in_specs=[SMEM, HBM, VMEM],
        out_specs=[VMEM] * inner,
        out_shape=[
            jax.ShapeDtypeStruct((count // inner, rows, width), jnp.bfloat16 if dx else jnp.float32)
            for dx in range(inner)
        ],
        scratch_shapes=[
            pltpu.VMEM((count, depth, width), weights.dtype),
            pltpu.SemaphoreType.DMA((count,)),
        ],
        compiler_params=params(),
        cost_estimate=cost(2 * rows * weights.size, 2 * weights.size),
        name="partials",
    )(scalars(active, *picks), in_hbm(weights), inputs)


def added(active, own, arrived):
    count, rows, width = own.shape

    def body(active_ref, own_ref, *refs):
        arrived_refs, out_refs = refs[: len(arrived)], refs[len(arrived) :]

        @pl.when(active_ref[0] == 1)
        def _():
            for n in range(count):
                total = own_ref[n]
                for ref in arrived_refs:
                    total = total + ref[n].astype(jnp.float32)
                out_refs[n][...] = total.astype(out_refs[n].dtype)

    return pl.pallas_call(
        body,
        in_specs=[SMEM] + [VMEM] * (1 + len(arrived)),
        out_specs=[VMEM] * count,
        out_shape=[
            jax.ShapeDtypeStruct((rows, width), jnp.bfloat16 if n else jnp.float32)
            for n in range(count)
        ],
        compiler_params=params(),
        cost_estimate=cost(own.size, 8 * own.size),
        name="added",
    )(scalars(active), own, *arrived)


def mean_square(upper, rot_out, low, high, picks, micro, seq):
    _, rows, width = low[0].shape
    eig_rows = rot_out.shape[1]
    count, inner = len(picks), len(low)

    def body(at, rot_ref, *refs):
        low_refs, high_refs = refs[:inner], refs[inner : 2 * inner]
        eig_ref, turned, block, result, sems = refs[2 * inner :]
        for m in range(micro):
            turned[m] = rot_ref[m * seq : (m + 1) * seq, :].T

        def copy(n):
            return pltpu.make_async_copy(
                result.at[n % 2], run_of(eig_ref, 1, at[1 + n], width), sems.at[n % 2]
            )

        def squared(m):
            product = jnp.dot(
                turned[m], block[m * seq : (m + 1) * seq, :], preferred_element_type=jnp.float32
            )
            return product * product

        for n in range(count):

            @pl.when(at[0] == 1)
            def _():
                block[...] = high_refs[n % inner][n // inner]

            @pl.when(at[0] == 0)
            def _():
                block[...] = low_refs[n % inner][n // inner]

            if n >= 2:
                copy(n - 2).wait()
            for m in range(0, micro, 2):
                pair = squared(m) + squared(m + 1) if m + 1 < micro else squared(m)
                result[n % 2] = pair if m == 0 else result[n % 2] + pair
            result[n % 2] = result[n % 2] * (1.0 / (seq * micro))
            copy(n).start()
        for n in range(max(0, count - 2), count):
            copy(n).wait()

    return pl.pallas_call(
        body,
        in_specs=[SMEM] + [VMEM] * (1 + 2 * inner),
        out_specs=HBM,
        out_shape=jax.ShapeDtypeStruct((eig_rows, count * width), jnp.float32),
        scratch_shapes=[
            pltpu.VMEM((micro, eig_rows, seq), rot_out.dtype),
            pltpu.VMEM((rows, width), rot_out.dtype),
            pltpu.VMEM((2, eig_rows, width), jnp.float32),
            pltpu.SemaphoreType.DMA((2,)),
        ],
        compiler_params=params(),
        cost_estimate=cost(16 * rows * eig_rows * count * width, 4 * eig_rows * count * width),
        name="mean_square",
    )(scalars(upper, *picks), rot_out, *low, *high)


def per_device(activations, top_grad, projection, basis_out, basis_in):
    sections = lax.axis_size("section")
    shards = lax.axis_size("shard")
    section, shard = lax.axis_index("section"), lax.axis_index("shard")
    micro, seq, feat_loc = top_grad.shape
    rows = micro * seq
    inputs = activations[0].reshape(rows, feat_loc)
    top = top_grad.reshape(rows, feat_loc)
    out_cols = basis_out[0]
    half = sections // 2

    inner = 1
    while 2 * (2 * inner) ** 2 <= shards:
        inner *= 2
    outer = shards // inner
    picks = [shard ^ part for part in range(shards)]

    def moved(block, flip, pairs):
        route = [(a * shards + i, b * shards + (i ^ flip)) for a, b in pairs for i in range(shards)]
        return lax.ppermute(block, ("section", "shard"), route)

    def spread(block, pairs):
        powers = [1 << p for p in range(outer.bit_length() - 1)]
        near = {dz: moved(block, dz * inner, pairs) for dz in reversed(powers)}
        return near, {dx: moved(block, dx, pairs) for dx in range(1, inner)}

    def along_outer(near, pairs):
        got = dict(near)
        for dz in range(outer):
            low = dz & -dz
            if dz not in got:
                got[dz] = moved(got[dz ^ low], low * inner, pairs)
        return got

    def handed_down(grad, turn):
        own = moved(grad, 0, [(turn + 1, turn)])
        if turn % 2 == 0:
            near, side = spread(grad, [(turn + 1, turn)])
        else:
            near, side = spread(own, [(turn, turn)])
        return {0: own, **near}, side

    def chain(sent, turns, rot_out, weights):
        for turn in turns:
            mine = section == turn
            near, side = sent
            got = along_outer(near, [(turn, turn)])
            base, rot_out = lax.optimization_barrier((near[0], rot_out))

            def product(dots, base, last):
                blocks, parts = [b for b, _ in dots], [p for _, p in dots]
                out_type = jnp.bfloat16 if last else jnp.float32
                if turn == 0:
                    at = [picks[p] for p in parts]
                    return stream_dot(mine, blocks, out_cols, at, base, out_type, False)
                return block_dot(mine, blocks, weights, parts, base, out_type)

            if turn == 0:
                base = jnp.zeros((rows, out_cols.shape[1]), jnp.float32)
                base, rot_out = lax.optimization_barrier((base, rot_out))
            blocks = {(0, 0): near[0], **{(0, dx): block for dx, block in side.items()}}
            totals = [product([(b, dx) for (_, dx), b in blocks.items()], base, outer == 1)]
            for dz in range(1, outer + 1):
                if dz < outer:
                    block, _ = lax.optimization_barrier((got[dz], totals[max(0, dz - 2)]))
                    blocks[dz, 0] = got[dz]
                    for dx in range(1, inner):
                        blocks[dz, dx] = moved(block, dx, [(turn, turn)])
                if dz > 1:
                    dots = [(blocks[dz - 1, dx], (dz - 1) * inner + dx) for dx in range(inner)]
                    if dz == outer - 1:
                        dots.append((blocks[dz, 0], dz * inner))
                    if dz == outer and outer > 2 and inner > 1:
                        dots = dots[1:]
                    totals.append(product(dots, totals[-1], dz == outer))
            if turn == 0:
                return jnp.where(mine, totals[-1], rot_out)
            sent = handed_down(totals[-1], turn - 1)
            parts = list(blocks)
            rot_out = stream_dot(
                mine,
                [blocks[p] for p in parts],
                out_cols,
                [picks[dz * inner + dx] for dz, dx in parts],
                rot_out,
                jnp.bfloat16,
                True,
            )
        return sent, rot_out

    def rotate_in(inputs, among):
        pairs = [(a, a) for a in among]
        mine = (section >= min(among)) & (section <= max(among))
        own, *others = partials(mine, inputs, basis_in[0], picks, inner)
        arrived = [moved(other, 1 + n, pairs) for n, other in enumerate(others)]
        own, *sums = added(mine, own, arrived)
        for dz, part in enumerate(sums, 1):
            own = own + moved(part, dz * inner, pairs).astype(jnp.float32)
        own = own.astype(jnp.bfloat16)
        powers = [1 << p for p in range(outer.bit_length() - 1)]
        near = {0: own, **{dz: moved(own, dz * inner, pairs) for dz in reversed(powers)}}
        got = along_outer(near, pairs)
        column = jnp.stack([got[dz] for dz in range(outer)])
        return [column] + [moved(column, dx, pairs) for dx in range(1, inner)]

    upper = list(range(sections - 1, half - 1, -1))
    lower = list(range(half - 1, -1, -1))
    rot_out = jnp.zeros((rows, out_cols.shape[1]), jnp.bfloat16)

    near, side = spread(top, [(upper[0], upper[0])])
    weights = resident(projection[0], picks)
    sent, rot_out = chain(({0: top, **near}, side), upper, rot_out, weights)
    low = rotate_in(inputs, lower)
    sent, low, inputs = lax.optimization_barrier((sent, low, inputs))
    rot_out = chain(sent, lower, rot_out, weights)
    high = rotate_in(inputs, upper)
    return mean_square(section >= half, rot_out, low, high, picks, micro, seq)[None]


def solution(mesh):
    return jax.shard_map(
        per_device,
        mesh=mesh,
        in_specs=(
            P("section", None, None, "shard"),
            P(None, None, "shard"),
            P("section", None, "shard"),
            P("section", None, "shard"),
            P("section", "shard", None),
        ),
        out_specs=P("section", "shard", None),
        check_vma=False,
    )
```

```python
import jax
import jax.numpy as jnp
from jax import lax
from jax.experimental import pallas as pl
from jax.experimental.pallas import tpu as pltpu
from jax.sharding import PartitionSpec as P

DOT_VMEM = 24 * 1024 * 1024
VMEM = pl.BlockSpec(memory_space=pltpu.VMEM)
SMEM = pl.BlockSpec(memory_space=pltpu.SMEM)
HBM = pl.BlockSpec(memory_space=pltpu.HBM)


def scalars(*values):
    return jnp.stack([jnp.asarray(v).astype(jnp.int32) for v in values])


def params():
    return pltpu.CompilerParams(vmem_limit_bytes=DOT_VMEM)


def cost(flops, moved):
    return pl.CostEstimate(flops=flops, bytes_accessed=moved, transcendentals=0)


def in_hbm(array):
    return pltpu.with_memory_space_constraint(array, pltpu.HBM)


def run_of(ref, axis, at, length):
    part = pl.ds(pl.multiple_of(at * length, length), length)
    return ref.at[part, :] if axis == 0 else ref.at[:, part]


def stream_dot(active, blocks, matrices, picks, bases, out_types):
    rows, depth = blocks[0].shape
    count, kinds = len(blocks), len(matrices)
    shapes = [m.shape[1] for m in matrices]
    given = [base for base in bases if base is not None]

    def body(at, *refs):
        refs = list(refs)

        def take(n):
            taken, refs[:n] = refs[:n], []
            return taken

        matrix_refs, block_refs = take(kinds), take(count)
        base_refs = [None if base is None else take(1)[0] for base in bases]
        out_refs, run_refs, total_refs, (sems,) = take(kinds), take(kinds), take(kinds), refs

        def copy(k, m):
            return pltpu.make_async_copy(
                run_of(matrix_refs[m], 0, at[1 + k], depth), run_refs[m].at[k], sems.at[m, k]
            )

        @pl.when(at[0] == 1)
        def _():
            for k in range(count):
                for m in range(kinds):
                    copy(k, m).start()
            for k in range(count):
                for m in range(kinds):
                    copy(k, m).wait()
                    width = 256 if shapes[m] % 256 == 0 else shapes[m]

                    def tile(j, _):
                        here = pl.ds(pl.multiple_of(j * width, width), width)
                        total = jnp.dot(
                            block_refs[k][...],
                            run_refs[m][k, :, here],
                            preferred_element_type=jnp.float32,
                        )
                        if k:
                            total += total_refs[m][:, here]
                        elif base_refs[m] is not None:
                            total += base_refs[m][:, here].astype(jnp.float32)
                        if k < count - 1:
                            total_refs[m][:, here] = total
                        else:
                            out_refs[m][:, here] = total.astype(out_types[m])
                        return 0

                    lax.fori_loop(0, shapes[m] // width, tile, 0)

    return pl.pallas_call(
        body,
        in_specs=[SMEM] + [HBM] * kinds + [VMEM] * (count + len(given)),
        out_specs=[VMEM] * kinds,
        out_shape=[jax.ShapeDtypeStruct((rows, n), t) for n, t in zip(shapes, out_types)],
        scratch_shapes=[pltpu.VMEM((count, depth, n), m.dtype) for n, m in zip(shapes, matrices)]
        + [pltpu.VMEM((rows, n), jnp.float32) for n in shapes]
        + [pltpu.SemaphoreType.DMA((kinds, count))],
        compiler_params=params(),
        cost_estimate=cost(
            2 * count * rows * depth * sum(shapes), 2 * count * depth * sum(shapes)
        ),
        name="stream_dot",
    )(scalars(active, *picks), *[in_hbm(m) for m in matrices], *blocks, *given)


def partials(active, inputs, weights, picks, inner):
    rows, depth = inputs.shape
    count = len(picks)
    width = weights.shape[1] // count

    def body(at, weights_ref, inputs_ref, *refs):
        out_refs, (runs, sems) = refs[:inner], refs[inner:]
        order = [n for dx in [*range(1, inner), 0] for n in range(dx, count, inner)]

        def copy(n):
            return pltpu.make_async_copy(
                run_of(weights_ref, 1, at[1 + n], width), runs.at[n], sems.at[n]
            )

        @pl.when(at[0] == 1)
        def _():
            for n in order:
                copy(n).start()
            for n in order:
                copy(n).wait()
                total = jnp.dot(inputs_ref[...], runs[n], preferred_element_type=jnp.float32)
                out_ref = out_refs[n % inner]
                out_ref[n // inner] = total.astype(out_ref.dtype)

    return pl.pallas_call(
        body,
        in_specs=[SMEM, HBM, VMEM],
        out_specs=[VMEM] * inner,
        out_shape=[
            jax.ShapeDtypeStruct((count // inner, rows, width), jnp.bfloat16 if dx else jnp.float32)
            for dx in range(inner)
        ],
        scratch_shapes=[
            pltpu.VMEM((count, depth, width), weights.dtype),
            pltpu.SemaphoreType.DMA((count,)),
        ],
        compiler_params=params(),
        cost_estimate=cost(2 * rows * weights.size, 2 * weights.size),
        name="partials",
    )(scalars(active, *picks), in_hbm(weights), inputs)


def added(active, own, arrived):
    count, rows, width = own.shape

    def body(active_ref, own_ref, *refs):
        arrived_refs, out_refs = refs[: len(arrived)], refs[len(arrived) :]

        @pl.when(active_ref[0] == 1)
        def _():
            for n in range(count):
                total = own_ref[n]
                for ref in arrived_refs:
                    total = total + ref[n].astype(jnp.float32)
                out_refs[n][...] = total.astype(out_refs[n].dtype)

    return pl.pallas_call(
        body,
        in_specs=[SMEM] + [VMEM] * (1 + len(arrived)),
        out_specs=[VMEM] * count,
        out_shape=[
            jax.ShapeDtypeStruct((rows, width), jnp.bfloat16 if n else jnp.float32)
            for n in range(count)
        ],
        compiler_params=params(),
        cost_estimate=cost(own.size, 8 * own.size),
        name="added",
    )(scalars(active), own, *arrived)


def mean_square(section, half, rot_outs, low, high, picks, micro, seq):
    _, rows, width = low[0].shape
    eig_rows = rot_outs[0].shape[1]
    count, inner, sections = len(picks), len(low), len(rot_outs)

    def body(at, *refs):
        rot_refs, refs = refs[:sections], refs[sections:]
        low_refs, high_refs = refs[:inner], refs[inner : 2 * inner]
        eig_ref, rot, block, result, sems = refs[2 * inner :]
        for s in range(sections):

            @pl.when(at[0] == s)
            def _():
                rot[...] = rot_refs[s][...]

        def copy(n):
            return pltpu.make_async_copy(
                result.at[n % 2], run_of(eig_ref, 1, at[1 + n], width), sems.at[n % 2]
            )

        for n in range(count):

            @pl.when(at[0] >= half)
            def _():
                block[...] = high_refs[n % inner][n // inner]

            @pl.when(at[0] < half)
            def _():
                block[...] = low_refs[n % inner][n // inner]

            if n >= 2:
                copy(n - 2).wait()
            for m in range(micro):
                rows_of = slice(m * seq, (m + 1) * seq)
                product = lax.dot_general(
                    rot[rows_of, :],
                    block[rows_of, :],
                    (((0,), (0,)), ((), ())),
                    preferred_element_type=jnp.float32,
                )
                square = product * product
                result[n % 2] = square if m == 0 else result[n % 2] + square
            result[n % 2] = result[n % 2] * (1.0 / (seq * micro))
            copy(n).start()
        for n in range(max(0, count - 2), count):
            copy(n).wait()

    return pl.pallas_call(
        body,
        in_specs=[SMEM] + [VMEM] * (sections + 2 * inner),
        out_specs=HBM,
        out_shape=jax.ShapeDtypeStruct((eig_rows, count * width), jnp.float32),
        scratch_shapes=[
            pltpu.VMEM((rows, eig_rows), rot_outs[0].dtype),
            pltpu.VMEM((rows, width), rot_outs[0].dtype),
            pltpu.VMEM((2, eig_rows, width), jnp.float32),
            pltpu.SemaphoreType.DMA((2,)),
        ],
        compiler_params=params(),
        cost_estimate=cost(16 * rows * eig_rows * count * width, 4 * eig_rows * count * width),
        name="mean_square",
    )(scalars(section, *picks), *rot_outs, *low, *high)


def per_device(activations, top_grad, projection, basis_out, basis_in):
    sections = lax.axis_size("section")
    shards = lax.axis_size("shard")
    section, shard = lax.axis_index("section"), lax.axis_index("shard")
    micro, seq, feat_loc = top_grad.shape
    rows = micro * seq
    inputs = activations[0].reshape(rows, feat_loc)
    top = top_grad.reshape(rows, feat_loc)
    weights, out_cols = projection[0], basis_out[0]
    half = sections // 2

    inner = 1
    while 2 * (2 * inner) ** 2 <= shards:
        inner *= 2
    outer = shards // inner
    picks = [shard ^ part for part in range(shards)]

    def moved(block, flip, pairs):
        route = [(a * shards + i, b * shards + (i ^ flip)) for a, b in pairs for i in range(shards)]
        return lax.ppermute(block, ("section", "shard"), route)

    def spread(block, pairs):
        powers = [1 << p for p in range(outer.bit_length() - 1)]
        near = {dz: moved(block, dz * inner, pairs) for dz in reversed(powers)}
        return near, {dx: moved(block, dx, pairs) for dx in range(1, inner)}

    def along_outer(near, pairs):
        got = dict(near)
        for dz in range(outer):
            low = dz & -dz
            if dz not in got:
                got[dz] = moved(got[dz ^ low], low * inner, pairs)
        return got

    def handed_down(grad, turn):
        own = moved(grad, 0, [(turn + 1, turn)])
        if turn % 2 == 0:
            near, side = spread(grad, [(turn + 1, turn)])
        else:
            near, side = spread(own, [(turn, turn)])
        return {0: own, **near}, side

    def relay(turn, sent, first=None):
        mine = section == turn
        near, side = sent
        got = along_outer(near, [(turn, turn)])
        matrices = [out_cols] if turn == 0 else [weights, out_cols]
        bases = [None] if turn == 0 else [near[0], None]

        def products(dots, bases, last):
            return stream_dot(
                mine,
                [block for block, _ in dots],
                matrices,
                [picks[part] for _, part in dots],
                bases,
                [jnp.bfloat16 if last else jnp.float32] * len(matrices),
            )

        blocks = {(0, 0): near[0], **{(0, dx): block for dx, block in side.items()}}
        if first is not None:
            blocks[0, 0], first = lax.optimization_barrier((near[0], first))
        dots = [(block, dx) for (_, dx), block in blocks.items()]
        totals = [products(dots, bases, outer == 1)]
        for dz in range(1, outer + 1):
            if dz < outer:
                block, _ = lax.optimization_barrier((got[dz], totals[max(0, dz - 2)][0]))
                blocks[dz, 0] = got[dz]
                for dx in range(1, inner):
                    blocks[dz, dx] = moved(block, dx, [(turn, turn)])
            if dz > 1:
                dots = [(blocks[dz - 1, dx], (dz - 1) * inner + dx) for dx in range(inner)]
                if dz == outer - 1:
                    dots.append((blocks[dz, 0], dz * inner))
                if dz == outer and outer > 2 and inner > 1:
                    dots = dots[1:]
                totals.append(products(dots, totals[-1], dz == outer))
        return totals[-1]

    def rotate_begin(inputs, among):
        pairs = [(a, a) for a in among]
        own, *others = partials(in_turn(among), inputs, basis_in[0], picks, inner)
        return own, others, [moved(other, 1 + n, pairs) for n, other in enumerate(others)]

    def rotate_end(own, arrived, among):
        pairs = [(a, a) for a in among]
        own, *sums = added(in_turn(among), own, arrived)
        for dz, part in enumerate(sums, 1):
            own = own + moved(part, dz * inner, pairs).astype(jnp.float32)
        own = own.astype(jnp.bfloat16)
        powers = [1 << p for p in range(outer.bit_length() - 1)]
        near = {0: own, **{dz: moved(own, dz * inner, pairs) for dz in reversed(powers)}}
        got = along_outer(near, pairs)
        return jnp.stack([got[dz] for dz in range(outer)])

    def in_turn(among):
        return (section >= min(among)) & (section <= max(among))

    def all_columns(column, among):
        return [column] + [moved(column, dx, [(a, a) for a in among]) for dx in range(1, inner)]

    upper = list(range(sections - 1, half - 1, -1))
    lower = list(range(half - 1, -1, -1))
    rot_outs = [None] * sections

    low_own, low_others, low_arrived = rotate_begin(inputs, lower)
    near, side = spread(top, [(upper[0], upper[0])])
    sent = {0: top, **near}, side
    for turn in upper:
        grad, rot_outs[turn] = relay(turn, sent, low_others if turn == upper[0] else None)
        if turn != upper[-1]:
            sent = handed_down(grad, turn - 1)
    low = rotate_end(low_own, low_arrived, lower)
    grad, low = lax.optimization_barrier((grad, low))
    sent = handed_down(grad, lower[0])
    low = all_columns(low, lower)
    inputs, _ = lax.optimization_barrier((inputs, sent[0][0]))
    high_own, _, high_arrived = rotate_begin(inputs, upper)
    for turn in lower:
        *grad, rot_outs[turn] = relay(turn, sent)
        if turn != 0:
            sent = handed_down(grad[0], turn - 1)
    high = all_columns(rotate_end(high_own, high_arrived, upper), upper)
    return mean_square(section, half, rot_outs, low, high, picks, micro, seq)[None]


def solution(mesh):
    return jax.shard_map(
        per_device,
        mesh=mesh,
        in_specs=(
            P("section", None, None, "shard"),
            P(None, None, "shard"),
            P("section", None, "shard"),
            P("section", None, "shard"),
            P("section", "shard", None),
        ),
        out_specs=P("section", "shard", None),
        check_vma=False,
    )
```

```python
import jax
import jax.numpy as jnp
from jax import lax
from jax.experimental import pallas as pl
from jax.experimental.pallas import tpu as pltpu
from jax.sharding import PartitionSpec as P

VMEM = pl.BlockSpec(memory_space=pltpu.VMEM)
SMEM = pl.BlockSpec(memory_space=pltpu.SMEM)
HBM = pl.BlockSpec(memory_space=pltpu.HBM)


def params(megabytes):
    return pltpu.CompilerParams(vmem_limit_bytes=megabytes * 1024 * 1024)


def in_hbm(array):
    return pltpu.with_memory_space_constraint(array, pltpu.HBM)


def run_of(ref, axis, at, length):
    part = pl.ds(pl.multiple_of(at * length, length), length)
    return ref.at[part, :] if axis == 0 else ref.at[:, part]


def resident(at, weights):
    count = at.shape[0] - 1
    depth, cols = weights.shape[0] // count, weights.shape[1]

    def body(at, weights_ref, out_ref, sems):
        def copy(i):
            return pltpu.make_async_copy(
                run_of(weights_ref, 0, at[1 + i], depth), out_ref.at[i], sems.at[i]
            )

        for i in range(count):
            copy(i).start()
        for i in range(count):
            copy(i).wait()

    return pl.pallas_call(
        body,
        in_specs=[SMEM, HBM],
        out_specs=VMEM,
        out_shape=jax.ShapeDtypeStruct((count, depth, cols), weights.dtype),
        scratch_shapes=[pltpu.SemaphoreType.DMA((count,))],
        compiler_params=params(4),
        name="resident",
    )(at, in_hbm(weights))


def block_dot(at, turn, blocks, weights, parts, base, out_type):
    rows, depth = blocks[0].shape
    cols = weights.shape[2]
    width = 256 if cols % 256 == 0 else cols
    count = len(blocks)

    def body(at, weights_ref, base_ref, *refs):
        @pl.when(at[0] == turn)
        def _():
            def tile(j, _):
                here = pl.ds(pl.multiple_of(j * width, width), width)
                total = base_ref[:, here].astype(jnp.float32)
                for block_ref, part in zip(refs[:count], parts):
                    total += jnp.dot(
                        block_ref[...],
                        weights_ref[part, :, here],
                        preferred_element_type=jnp.float32,
                    )
                refs[count][:, here] = total.astype(out_type)
                return 0

            lax.fori_loop(0, cols // width, tile, 0)

    return pl.pallas_call(
        body,
        in_specs=[SMEM] + [VMEM] * (count + 2),
        out_specs=VMEM,
        out_shape=jax.ShapeDtypeStruct((rows, cols), out_type),
        compiler_params=params(4),
        name="block_dot",
    )(at, weights, base, *blocks)


def stream_dot(at, turn, blocks, weights, parts, base, out_type):
    rows, depth = blocks[0].shape
    cols = weights.shape[1]
    count = len(blocks)

    def body(at, weights_ref, *refs):
        block_refs, (out_ref, runs, sems) = refs[:count], refs[-3:]

        def copy(k):
            return pltpu.make_async_copy(
                run_of(weights_ref, 0, at[1 + parts[k]], depth), runs.at[k], sems.at[k]
            )

        @pl.when(at[0] == turn)
        def _():
            for k in range(count):
                copy(k).start()
            total = None if base is None else refs[count][...]
            for k in range(count):
                copy(k).wait()
                part = jnp.dot(block_refs[k][...], runs[k], preferred_element_type=jnp.float32)
                total = part if total is None else total + part
            out_ref[...] = total.astype(out_type)

    return pl.pallas_call(
        body,
        in_specs=[SMEM, HBM] + [VMEM] * (count + (base is not None)),
        out_specs=VMEM,
        out_shape=jax.ShapeDtypeStruct((rows, cols), out_type),
        scratch_shapes=[
            pltpu.VMEM((count, depth, cols), weights.dtype),
            pltpu.SemaphoreType.DMA((count,)),
        ],
        compiler_params=params(14),
        name="stream_dot",
    )(at, in_hbm(weights), *blocks, *([] if base is None else [base]))


def partials(at, among, inputs, weights, inner):
    rows, depth = inputs.shape
    count = at.shape[0] - 1
    width = weights.shape[1] // count

    def body(at, weights_ref, inputs_ref, *refs):
        out_refs, (runs, sems) = refs[:inner], refs[inner:]
        order = [n for dx in [*range(1, inner), 0] for n in range(dx, count, inner)]

        def copy(n):
            return pltpu.make_async_copy(
                run_of(weights_ref, 1, at[1 + n], width), runs.at[n], sems.at[n]
            )

        @pl.when((at[0] >= min(among)) & (at[0] <= max(among)))
        def _():
            for n in order:
                copy(n).start()
            for n in order:
                copy(n).wait()
                total = jnp.dot(inputs_ref[...], runs[n], preferred_element_type=jnp.float32)
                out_ref = out_refs[n % inner]
                out_ref[n // inner] = total.astype(out_ref.dtype)

    return pl.pallas_call(
        body,
        in_specs=[SMEM, HBM, VMEM],
        out_specs=[VMEM] * inner,
        out_shape=[
            jax.ShapeDtypeStruct((count // inner, rows, width), jnp.bfloat16 if dx else jnp.float32)
            for dx in range(inner)
        ],
        scratch_shapes=[
            pltpu.VMEM((count, depth, width), weights.dtype),
            pltpu.SemaphoreType.DMA((count,)),
        ],
        compiler_params=params(14),
        name="partials",
    )(at, in_hbm(weights), inputs)


def added(at, among, own, arrived):
    count, rows, width = own.shape

    def body(at, own_ref, *refs):
        arrived_refs, out_refs = refs[: len(arrived)], refs[len(arrived) :]

        @pl.when((at[0] >= min(among)) & (at[0] <= max(among)))
        def _():
            for n in range(count):
                total = own_ref[n]
                for ref in arrived_refs:
                    total = total + ref[n].astype(jnp.float32)
                out_refs[n][...] = total.astype(out_refs[n].dtype)

    return pl.pallas_call(
        body,
        in_specs=[SMEM] + [VMEM] * (1 + len(arrived)),
        out_specs=[VMEM] * count,
        out_shape=[
            jax.ShapeDtypeStruct((rows, width), jnp.bfloat16 if n else jnp.float32)
            for n in range(count)
        ],
        compiler_params=params(4),
        name="added",
    )(at, own, *arrived)


def mean_square(at, half, rot_outs, low, high, micro, seq):
    _, rows, width = low[0].shape
    eig_rows = rot_outs[0].shape[1]
    count, inner, sections = at.shape[0] - 1, len(low), len(rot_outs)

    def body(at, *refs):
        rot_refs, refs = refs[:sections], refs[sections:]
        low_refs, high_refs = refs[:inner], refs[inner : 2 * inner]
        eig_ref, rot, block, result, sems = refs[2 * inner :]
        for s in range(sections):

            @pl.when(at[0] == s)
            def _():
                rot[...] = rot_refs[s][...]

        def copy(n):
            return pltpu.make_async_copy(
                result.at[n % 2], run_of(eig_ref, 1, at[1 + n], width), sems.at[n % 2]
            )

        for n in range(count):

            @pl.when(at[0] >= half)
            def _():
                block[...] = high_refs[n % inner][n // inner]

            @pl.when(at[0] < half)
            def _():
                block[...] = low_refs[n % inner][n // inner]

            if n >= 2:
                copy(n - 2).wait()
            for m in range(micro):
                rows_of = slice(m * seq, (m + 1) * seq)
                product = lax.dot_general(
                    rot[rows_of, :],
                    block[rows_of, :],
                    (((0,), (0,)), ((), ())),
                    preferred_element_type=jnp.float32,
                )
                square = product * product
                total = square if m == 0 else result[n % 2] + square
                result[n % 2] = total if m < micro - 1 else total * (1.0 / (seq * micro))
            copy(n).start()
        for n in range(max(0, count - 2), count):
            copy(n).wait()

    return pl.pallas_call(
        body,
        in_specs=[SMEM] + [VMEM] * (sections + 2 * inner),
        out_specs=HBM,
        out_shape=jax.ShapeDtypeStruct((eig_rows, count * width), jnp.float32),
        scratch_shapes=[
            pltpu.VMEM((rows, eig_rows), rot_outs[0].dtype),
            pltpu.VMEM((rows, width), rot_outs[0].dtype),
            pltpu.VMEM((2, eig_rows, width), jnp.float32),
            pltpu.SemaphoreType.DMA((2,)),
        ],
        compiler_params=params(14),
        name="mean_square",
    )(at, *rot_outs, *low, *high)


def per_device(activations, top_grad, projection, basis_out, basis_in):
    sections = lax.axis_size("section")
    shards = lax.axis_size("shard")
    micro, seq, feat_loc = top_grad.shape
    rows = micro * seq
    inputs = activations[0].reshape(rows, feat_loc)
    top = top_grad.reshape(rows, feat_loc)
    weights, out_cols = projection[0], basis_out[0]
    half = sections // 2

    inner = 1
    while 2 * (2 * inner) ** 2 <= shards:
        inner *= 2
    outer = shards // inner
    shard = lax.axis_index("shard")
    at = jnp.stack(
        [jnp.int32(lax.axis_index("section"))] + [jnp.int32(shard ^ p) for p in range(shards)]
    )

    def moved(block, flip, pairs):
        route = [(a * shards + i, b * shards + (i ^ flip)) for a, b in pairs for i in range(shards)]
        return lax.ppermute(block, ("section", "shard"), route)

    def spread(block, pairs):
        powers = [1 << p for p in range(outer.bit_length() - 1)]
        near = {dz: moved(block, dz * inner, pairs) for dz in reversed(powers)}
        return near, {dx: moved(block, dx, pairs) for dx in range(1, inner)}

    def along_outer(near, pairs):
        got = dict(near)
        for dz in range(outer):
            low = dz & -dz
            if dz not in got:
                got[dz] = moved(got[dz ^ low], low * inner, pairs)
        return got

    def handed_down(grad, turn):
        own = moved(grad, 0, [(turn + 1, turn)])
        if turn % 2 == 0:
            near, side = spread(grad, [(turn + 1, turn)])
        else:
            near, side = spread(own, [(turn, turn)])
        return {0: own, **near}, side

    def relay(turn, sent, before, within):
        near, side = sent
        got = along_outer(near, [(turn, turn)])
        start, *_ = lax.optimization_barrier((near[0], *before))

        def products(dots, base, last):
            blocks, parts = [block for block, _ in dots], [part for _, part in dots]
            out_type = jnp.bfloat16 if last else jnp.float32
            if turn == 0:
                return stream_dot(at, turn, blocks, out_cols, parts, base, out_type)
            return block_dot(at, turn, blocks, weights, parts, base, out_type)

        blocks = {(0, 0): start, **{(0, dx): block for dx, block in side.items()}}
        dots = [(block, dx) for (_, dx), block in blocks.items()]
        totals = [products(dots, None if turn == 0 else start, outer == 1)]
        for dz in range(1, outer + 1):
            if dz < outer:
                block, *_ = lax.optimization_barrier(
                    (got[dz], totals[max(0, dz - 2)], *(within if dz == outer - 1 else []))
                )
                blocks[dz, 0] = got[dz]
                for dx in range(1, inner):
                    blocks[dz, dx] = moved(block, dx, [(turn, turn)])
            if dz > 1:
                dots = [(blocks[dz - 1, dx], (dz - 1) * inner + dx) for dx in range(inner)]
                if dz == outer - 1:
                    dots.append((blocks[dz, 0], dz * inner))
                if dz == outer and outer > 2 and inner > 1:
                    dots = dots[1:]
                totals.append(products(dots, totals[-1], dz == outer))
        return totals[-1], blocks

    def rotated(turn, blocks):
        parts = [dz * inner + dx for dz, dx in blocks]
        return stream_dot(at, turn, list(blocks.values()), out_cols, parts, None, jnp.bfloat16)

    def rotate_begin(inputs, among):
        pairs = [(a, a) for a in among]
        own, *others = partials(at, among, inputs, basis_in[0], inner)
        return own, others, [moved(other, 1 + n, pairs) for n, other in enumerate(others)]

    def summed(sums, among):
        pairs = [(a, a) for a in among]
        own = sums[0]
        for dz, part in enumerate(sums[1:], 1):
            own = own + moved(part, dz * inner, pairs).astype(jnp.float32)
        return own.astype(jnp.bfloat16)

    def outer_columns(own, among):
        pairs = [(a, a) for a in among]
        powers = [1 << p for p in range(outer.bit_length() - 1)]
        near = {0: own, **{dz: moved(own, dz * inner, pairs) for dz in reversed(powers)}}
        got = along_outer(near, pairs)
        return jnp.stack([got[dz] for dz in range(outer)])

    def all_columns(column, among):
        return [column] + [moved(column, dx, [(a, a) for a in among]) for dx in range(1, inner)]

    upper = list(range(sections - 1, half - 1, -1))
    lower = list(range(half - 1, -1, -1))
    rot_outs = [None] * sections

    low_own, low_others, low_arrived = rotate_begin(inputs, lower)
    near, side = spread(top, [(upper[0], upper[0])])
    weights = resident(at, weights)
    sums = added(at, lower, low_own, low_arrived)
    low = summed(sums, lower)
    sent, before, within = ({0: top, **near}, side), low_others, sums
    for turn in upper:
        grad, blocks = relay(turn, sent, before, within)
        within = []
        if turn != upper[-1]:
            sent = handed_down(grad, turn - 1)
            rot_outs[turn] = rotated(turn, blocks)
            before = [rot_outs[turn], low]
    low = outer_columns(low, lower)
    grad, low = lax.optimization_barrier((grad, low))
    sent = handed_down(grad, lower[0])
    low = all_columns(low, lower)
    rot_outs[upper[-1]] = rotated(upper[-1], blocks)
    inputs, _ = lax.optimization_barrier((inputs, sent[0][0]))
    high_own, _, high_arrived = rotate_begin(inputs, upper)
    before = [rot_outs[upper[-1]], *low]
    for turn in lower:
        grad, blocks = relay(turn, sent, before, [])
        if turn != 0:
            sent = handed_down(grad, turn - 1)
            rot_outs[turn] = rotated(turn, blocks)
            before = [rot_outs[turn]]
    rot_outs[0] = grad
    sums = added(at, upper, high_own, high_arrived)
    high = all_columns(outer_columns(summed(sums, upper), upper), upper)
    return mean_square(at, half, rot_outs, low, high, micro, seq)[None]


def solution(mesh):
    return jax.shard_map(
        per_device,
        mesh=mesh,
        in_specs=(
            P("section", None, None, "shard"),
            P(None, None, "shard"),
            P("section", None, "shard"),
            P("section", None, "shard"),
            P("section", "shard", None),
        ),
        out_specs=P("section", "shard", None),
        check_vma=False,
    )
```

```python
import jax
import jax.numpy as jnp
from jax import lax
from jax.experimental import pallas as pl
from jax.experimental.pallas import tpu as pltpu
from jax.sharding import PartitionSpec as P

VMEM = pl.BlockSpec(memory_space=pltpu.VMEM)
SMEM = pl.BlockSpec(memory_space=pltpu.SMEM)
HBM = pl.BlockSpec(memory_space=pltpu.HBM)


def params(megabytes):
    return pltpu.CompilerParams(vmem_limit_bytes=megabytes * 1024 * 1024)


def in_hbm(array):
    return pltpu.with_memory_space_constraint(array, pltpu.HBM)


def run_of(ref, axis, at, length):
    part = pl.ds(pl.multiple_of(at * length, length), length)
    return ref.at[part, :] if axis == 0 else ref.at[:, part]


def resident(at, weights, only=None):
    count = at.shape[0] - 1
    depth, cols = weights.shape[0] // count, weights.shape[1]

    def body(at, weights_ref, out_ref, sems):
        def copy(i):
            return pltpu.make_async_copy(
                run_of(weights_ref, 0, at[1 + i], depth), out_ref.at[i], sems.at[i]
            )

        @pl.when((at[0] == only) if only is not None else (at[0] >= 0))
        def _():
            for i in range(count):
                copy(i).start()
            for i in range(count):
                copy(i).wait()

    return pl.pallas_call(
        body,
        in_specs=[SMEM, HBM],
        out_specs=VMEM,
        out_shape=jax.ShapeDtypeStruct((count, depth, cols), weights.dtype),
        scratch_shapes=[pltpu.SemaphoreType.DMA((count,))],
        compiler_params=params(4),
        name="resident",
    )(at, in_hbm(weights))


def block_dot(at, turn, blocks, weights, parts, base, out_type):
    rows, depth = blocks[0].shape
    cols = weights.shape[2]
    width = 256 if cols % 256 == 0 else cols
    count = len(blocks)

    def body(at, weights_ref, *refs):
        @pl.when(at[0] == turn)
        def _():
            def tile(j, _):
                here = pl.ds(pl.multiple_of(j * width, width), width)
                total = None if base is None else refs[count][:, here].astype(jnp.float32)
                for block_ref, part in zip(refs[:count], parts):
                    product = jnp.dot(
                        block_ref[...],
                        weights_ref[part, :, here],
                        preferred_element_type=jnp.float32,
                    )
                    total = product if total is None else total + product
                refs[-1][:, here] = total.astype(out_type)
                return 0

            lax.fori_loop(0, cols // width, tile, 0)

    return pl.pallas_call(
        body,
        in_specs=[SMEM] + [VMEM] * (1 + count + (base is not None)),
        out_specs=VMEM,
        out_shape=jax.ShapeDtypeStruct((rows, cols), out_type),
        compiler_params=params(4),
        name="block_dot",
    )(at, weights, *blocks, *([] if base is None else [base]))


def stream_dot(at, turn, blocks, weights, parts, out_type):
    rows, depth = blocks[0].shape
    cols = weights.shape[1]
    count = len(blocks)

    def body(at, weights_ref, *refs):
        block_refs, (out_ref, runs, sems) = refs[:count], refs[-3:]

        def copy(k):
            return pltpu.make_async_copy(
                run_of(weights_ref, 0, at[1 + parts[k]], depth), runs.at[k], sems.at[k]
            )

        @pl.when(at[0] == turn)
        def _():
            for k in range(count):
                copy(k).start()
            total = None
            for k in range(count):
                copy(k).wait()
                part = jnp.dot(block_refs[k][...], runs[k], preferred_element_type=jnp.float32)
                total = part if total is None else total + part
            out_ref[...] = total.astype(out_type)

    return pl.pallas_call(
        body,
        in_specs=[SMEM, HBM] + [VMEM] * count,
        out_specs=VMEM,
        out_shape=jax.ShapeDtypeStruct((rows, cols), out_type),
        scratch_shapes=[
            pltpu.VMEM((count, depth, cols), weights.dtype),
            pltpu.SemaphoreType.DMA((count,)),
        ],
        compiler_params=params(14),
        name="stream_dot",
    )(at, in_hbm(weights), *blocks)


def partials(at, among, inputs, weights, inner, after):
    rows, depth = inputs.shape
    count = at.shape[0] - 1
    width = weights.shape[1] // count

    def body(at, weights_ref, inputs_ref, *refs):
        refs = refs[len(after) :]
        out_refs, (runs, sems) = refs[:inner], refs[inner:]
        order = [n for dx in [*range(1, inner), 0] for n in range(dx, count, inner)]

        def copy(n):
            return pltpu.make_async_copy(
                run_of(weights_ref, 1, at[1 + n], width), runs.at[n], sems.at[n]
            )

        @pl.when((at[0] >= min(among)) & (at[0] <= max(among)))
        def _():
            for n in order:
                copy(n).start()
            for n in order:
                copy(n).wait()
                total = jnp.dot(inputs_ref[...], runs[n], preferred_element_type=jnp.float32)
                out_ref = out_refs[n % inner]
                out_ref[n // inner] = total.astype(out_ref.dtype)

    return pl.pallas_call(
        body,
        in_specs=[SMEM, HBM, VMEM] + [VMEM] * len(after),
        out_specs=[VMEM] * inner,
        out_shape=[
            jax.ShapeDtypeStruct((count // inner, rows, width), jnp.bfloat16 if dx else jnp.float32)
            for dx in range(inner)
        ],
        scratch_shapes=[
            pltpu.VMEM((count, depth, width), weights.dtype),
            pltpu.SemaphoreType.DMA((count,)),
        ],
        compiler_params=params(14),
        name="partials",
    )(at, in_hbm(weights), inputs, *after)


def added(at, among, own, arrived):
    count, rows, width = own.shape

    def body(at, own_ref, *refs):
        arrived_refs, out_refs = refs[: len(arrived)], refs[len(arrived) :]

        @pl.when((at[0] >= min(among)) & (at[0] <= max(among)))
        def _():
            for n in range(count):
                total = own_ref[n]
                for ref in arrived_refs:
                    total = total + ref[n].astype(jnp.float32)
                out_refs[n][...] = total.astype(out_refs[n].dtype)

    return pl.pallas_call(
        body,
        in_specs=[SMEM] + [VMEM] * (1 + len(arrived)),
        out_specs=[VMEM] * count,
        out_shape=[
            jax.ShapeDtypeStruct((rows, width), jnp.bfloat16 if n else jnp.float32)
            for n in range(count)
        ],
        compiler_params=params(4),
        name="added",
    )(at, own, *arrived)


def mean_square(at, half, rot_outs, low, high, low_runs, high_runs, micro, seq):
    _, rows, width = low[0].shape
    eig_rows = rot_outs[0].shape[1]
    count, sections = len(low_runs), len(rot_outs)

    def body(at, *refs):
        rot_refs, refs = refs[:sections], refs[sections:]
        low_refs, refs = refs[: len(low)], refs[len(low) :]
        high_refs, refs = refs[: len(high)], refs[len(high) :]
        eig_ref, rot, block, result, sems = refs
        for s in range(sections):

            @pl.when(at[0] == s)
            def _():
                rot[...] = rot_refs[s][...]

        def copy(n):
            return pltpu.make_async_copy(
                result.at[n % 2], run_of(eig_ref, 1, at[1 + n], width), sems.at[n % 2]
            )

        for n in range(count):

            @pl.when(at[0] >= half)
            def _():
                a, i = high_runs[n]
                block[...] = high_refs[a][i]

            @pl.when(at[0] < half)
            def _():
                a, i = low_runs[n]
                block[...] = low_refs[a][i]

            if n >= 2:
                copy(n - 2).wait()
            for m in range(micro):
                rows_of = slice(m * seq, (m + 1) * seq)
                product = lax.dot_general(
                    rot[rows_of, :],
                    block[rows_of, :],
                    (((0,), (0,)), ((), ())),
                    preferred_element_type=jnp.float32,
                )
                square = product * product
                total = square if m == 0 else result[n % 2] + square
                result[n % 2] = total if m < micro - 1 else total * (1.0 / (seq * micro))
            copy(n).start()
        for n in range(max(0, count - 2), count):
            copy(n).wait()

    return pl.pallas_call(
        body,
        in_specs=[SMEM] + [VMEM] * (sections + len(low) + len(high)),
        out_specs=HBM,
        out_shape=jax.ShapeDtypeStruct((eig_rows, count * width), jnp.float32),
        scratch_shapes=[
            pltpu.VMEM((rows, eig_rows), rot_outs[0].dtype),
            pltpu.VMEM((rows, width), rot_outs[0].dtype),
            pltpu.VMEM((2, eig_rows, width), jnp.float32),
            pltpu.SemaphoreType.DMA((2,)),
        ],
        compiler_params=params(14),
        name="mean_square",
    )(at, *rot_outs, *low, *high)


def per_device(activations, top_grad, projection, basis_out, basis_in):
    sections = lax.axis_size("section")
    shards = lax.axis_size("shard")
    micro, seq, feat_loc = top_grad.shape
    rows = micro * seq
    inputs = activations[0].reshape(rows, feat_loc)
    top = top_grad.reshape(rows, feat_loc)
    weights, out_cols = projection[0], basis_out[0]
    half = sections // 2

    inner = 1
    while 2 * (2 * inner) ** 2 <= shards:
        inner *= 2
    outer = shards // inner
    shard = lax.axis_index("shard")
    at = jnp.stack(
        [jnp.int32(lax.axis_index("section"))] + [jnp.int32(shard ^ p) for p in range(shards)]
    )

    def moved(block, flip, pairs):
        route = [(a * shards + i, b * shards + (i ^ flip)) for a, b in pairs for i in range(shards)]
        return lax.ppermute(block, ("section", "shard"), route)

    def spread(block, pairs):
        powers = [1 << p for p in range(outer.bit_length() - 1)]
        near = {dz: moved(block, dz * inner, pairs) for dz in reversed(powers)}
        return near, {dx: moved(block, dx, pairs) for dx in range(1, inner)}

    def along_outer(near, pairs):
        got = dict(near)
        for dz in range(outer):
            low = dz & -dz
            if dz not in got:
                got[dz] = moved(got[dz ^ low], low * inner, pairs)
        return got

    def handed_down(grad, turn):
        own = moved(grad, 0, [(turn + 1, turn)])
        if turn % 2 == 0:
            near, side = spread(grad, [(turn + 1, turn)])
        else:
            near, side = spread(own, [(turn, turn)])
        return {0: own, **near}, side

    order = [0] + [1 << p for p in reversed(range(outer.bit_length() - 1))]
    order += [dz for dz in range(outer) if dz not in order]

    def relay(turn, sent, before, within, matrix):
        near, side = sent
        got = along_outer(near, [(turn, turn)])
        start, *_ = lax.optimization_barrier((near[0], *before))

        def products(dots, base, last):
            blocks, parts = [block for block, _ in dots], [part for _, part in dots]
            out_type = jnp.bfloat16 if last else jnp.float32
            return block_dot(at, turn, blocks, matrix, parts, base, out_type)

        blocks = {(0, 0): start, **{(0, dx): block for dx, block in side.items()}}
        dots = [(block, dx) for (_, dx), block in blocks.items()]
        totals = [products(dots, None if turn == 0 else start, outer == 1)]
        for n in range(1, outer + 1):
            if n < outer:
                dz = order[n]
                ties = [totals[0]] + [blocks[order[max(0, n - 2)], dx] for dx in range(1, inner)]
                block, *_ = lax.optimization_barrier(
                    (got[dz], *ties, *(within if n == outer - 1 else []))
                )
                blocks[dz, 0] = got[dz]
                for dx in range(1, inner):
                    blocks[dz, dx] = moved(block, dx, [(turn, turn)])
            if n > 1:
                dz = order[n - 1]
                dots = [(blocks[dz, dx], dz * inner + dx) for dx in range(inner)]
                if n == outer - 1:
                    dots.append((blocks[order[n], 0], order[n] * inner))
                if n == outer and outer > 2 and inner > 1:
                    dots = dots[1:]
                totals.append(products(dots, totals[-1], n == outer))
        return totals[-1], blocks

    def rotated(turn, blocks):
        parts = [dz * inner + dx for dz, dx in blocks]
        return stream_dot(at, turn, list(blocks.values()), out_cols, parts, jnp.bfloat16)

    def rotate_begin(inputs, among, after=()):
        pairs = [(a, a) for a in among]
        own, *others = partials(at, among, inputs, basis_in[0], inner, after)
        return own, others, [moved(other, 1 + n, pairs) for n, other in enumerate(others)]

    def summed(sums, among):
        pairs = [(a, a) for a in among]
        own = sums[0]
        for dz, part in enumerate(sums[1:], 1):
            own = own + moved(part, dz * inner, pairs).astype(jnp.float32)
        return own.astype(jnp.bfloat16)

    def outer_columns(own, among, halves):
        pairs = [(a, a) for a in among]
        powers = [1 << p for p in range(outer.bit_length() - 1)]
        near = {0: own, **{dz: moved(own, dz * inner, pairs) for dz in reversed(powers)}}
        got = along_outer(near, pairs)
        return [jnp.stack([got[dz] for dz in some]) for some in halves]

    def all_columns(columns, among):
        pairs = [(a, a) for a in among]
        return [[c] + [moved(c, dx, pairs) for dx in range(1, inner)] for c in columns]

    upper = list(range(sections - 1, half - 1, -1))
    lower = list(range(half - 1, -1, -1))
    rot_outs = [None] * sections

    low_own, low_others, low_arrived = rotate_begin(inputs, lower)
    near, side = spread(top, [(upper[0], upper[0])])
    weights = resident(at, weights)
    halves = [order]
    sums = added(at, lower, low_own, low_arrived)
    low = summed(sums, lower)
    sent, before, within = ({0: top, **near}, side), low_others, sums
    for turn in upper:
        grad, blocks = relay(turn, sent, before, within, weights)
        if turn != upper[-1]:
            sent = handed_down(grad, turn - 1)
            rot_outs[turn] = rotated(turn, blocks)
            before, within = [low], [rot_outs[turn]]
    low = outer_columns(low, lower, halves)
    grad, low = lax.optimization_barrier((grad, low))
    sent = handed_down(grad, lower[0])
    done = moved(grad[:16, :128], 0, [(upper[-1], a) for a in upper[:1]])
    low = all_columns(low, lower)
    rot_outs[upper[-1]] = rotated(upper[-1], blocks)
    inputs, *_ = lax.optimization_barrier((inputs, sent[0][0]))
    last_cols = resident(at, out_cols, 0)
    high_own, _, high_arrived = rotate_begin(inputs, upper, [done])
    before, within = [], [rot_outs[upper[-1]], *jax.tree.leaves(low)]
    for turn in lower:
        grad, blocks = relay(turn, sent, before, within, weights if turn else last_cols)
        if turn != 0:
            sent = handed_down(grad, turn - 1)
            rot_outs[turn] = rotated(turn, blocks)
            before, within = [], [rot_outs[turn]]
    rot_outs[0] = grad
    sums = added(at, upper, high_own, high_arrived)
    high = all_columns(outer_columns(summed(sums, upper), upper, [order]), upper)

    def runs(parts):
        place = {dz: (a, i) for a, some in enumerate(parts) for i, dz in enumerate(some)}
        return [(place[p // inner][0] * inner + p % inner, place[p // inner][1]) for p in range(shards)]

    low, high = jax.tree.leaves(low), jax.tree.leaves(high)
    return mean_square(
        at, half, rot_outs, low, high, runs(halves), runs([order]), micro, seq
    )[None]


def solution(mesh):
    return jax.shard_map(
        per_device,
        mesh=mesh,
        in_specs=(
            P("section", None, None, "shard"),
            P(None, None, "shard"),
            P("section", None, "shard"),
            P("section", None, "shard"),
            P("section", "shard", None),
        ),
        out_specs=P("section", "shard", None),
        check_vma=False,
    )
```

```python
import jax
import jax.numpy as jnp
from jax import lax
from jax.experimental import pallas as pl
from jax.experimental.pallas import tpu as pltpu
from jax.sharding import PartitionSpec as P

VMEM = pl.BlockSpec(memory_space=pltpu.VMEM)
SMEM = pl.BlockSpec(memory_space=pltpu.SMEM)
HBM = pl.BlockSpec(memory_space=pltpu.HBM)


def params(megabytes):
    return pltpu.CompilerParams(vmem_limit_bytes=megabytes * 1024 * 1024)


def in_hbm(array):
    return pltpu.with_memory_space_constraint(array, pltpu.HBM)


def run_of(ref, axis, at, length):
    part = pl.ds(pl.multiple_of(at * length, length), length)
    return ref.at[part, :] if axis == 0 else ref.at[:, part]


def resident(at, weights, only=None):
    count = at.shape[0] - 1
    depth, cols = weights.shape[0] // count, weights.shape[1]

    def body(at, weights_ref, out_ref, sems):
        def copy(i):
            return pltpu.make_async_copy(
                run_of(weights_ref, 0, at[1 + i], depth), out_ref.at[i], sems.at[i]
            )

        @pl.when((at[0] == only) if only is not None else (at[0] >= 0))
        def _():
            for i in range(count):
                copy(i).start()
            for i in range(count):
                copy(i).wait()

    return pl.pallas_call(
        body,
        in_specs=[SMEM, HBM],
        out_specs=VMEM,
        out_shape=jax.ShapeDtypeStruct((count, depth, cols), weights.dtype),
        scratch_shapes=[pltpu.SemaphoreType.DMA((count,))],
        compiler_params=params(4),
        name="resident",
    )(at, in_hbm(weights))


def block_dot(at, turn, blocks, weights, parts, base, out_type):
    rows, depth = blocks[0].shape
    cols = weights.shape[2]
    width = 256 if cols % 256 == 0 else cols
    count = len(blocks)

    def body(at, weights_ref, *refs):
        @pl.when(at[0] == turn)
        def _():
            def tile(j, _):
                here = pl.ds(pl.multiple_of(j * width, width), width)
                total = None if base is None else refs[count][:, here].astype(jnp.float32)
                for block_ref, part in zip(refs[:count], parts):
                    product = jnp.dot(
                        block_ref[...],
                        weights_ref[part, :, here],
                        preferred_element_type=jnp.float32,
                    )
                    total = product if total is None else total + product
                refs[-1][:, here] = total.astype(out_type)
                return 0

            lax.fori_loop(0, cols // width, tile, 0)

    return pl.pallas_call(
        body,
        in_specs=[SMEM] + [VMEM] * (1 + count + (base is not None)),
        out_specs=VMEM,
        out_shape=jax.ShapeDtypeStruct((rows, cols), out_type),
        compiler_params=params(4),
        name="block_dot",
    )(at, weights, *blocks, *([] if base is None else [base]))


def stream_dot(at, turn, blocks, weights, parts, out_type):
    rows, depth = blocks[0].shape
    cols = weights.shape[1]
    count = len(blocks)

    def body(at, weights_ref, *refs):
        block_refs, (out_ref, runs, sems) = refs[:count], refs[-3:]

        def copy(k):
            return pltpu.make_async_copy(
                run_of(weights_ref, 0, at[1 + parts[k]], depth), runs.at[k], sems.at[k]
            )

        @pl.when(at[0] == turn)
        def _():
            for k in range(count):
                copy(k).start()
            total = None
            for k in range(count):
                copy(k).wait()
                part = jnp.dot(block_refs[k][...], runs[k], preferred_element_type=jnp.float32)
                total = part if total is None else total + part
            out_ref[...] = total.astype(out_type)

    return pl.pallas_call(
        body,
        in_specs=[SMEM, HBM] + [VMEM] * count,
        out_specs=VMEM,
        out_shape=jax.ShapeDtypeStruct((rows, cols), out_type),
        scratch_shapes=[
            pltpu.VMEM((count, depth, cols), weights.dtype),
            pltpu.SemaphoreType.DMA((count,)),
        ],
        compiler_params=params(14),
        name="stream_dot",
    )(at, in_hbm(weights), *blocks)


def partials(at, among, inputs, weights, inner):
    rows, depth = inputs.shape
    count = at.shape[0] - 1
    width = weights.shape[1] // count

    def body(at, weights_ref, inputs_ref, *refs):
        out_refs, (runs, sems) = refs[:inner], refs[inner:]
        order = [n for dx in [*range(1, inner), 0] for n in range(dx, count, inner)]

        def copy(n):
            return pltpu.make_async_copy(
                run_of(weights_ref, 1, at[1 + n], width), runs.at[n], sems.at[n]
            )

        @pl.when((at[0] >= min(among)) & (at[0] <= max(among)))
        def _():
            for n in order:
                copy(n).start()
            for n in order:
                copy(n).wait()
                total = jnp.dot(inputs_ref[...], runs[n], preferred_element_type=jnp.float32)
                out_ref = out_refs[n % inner]
                out_ref[n // inner] = total.astype(out_ref.dtype)

    return pl.pallas_call(
        body,
        in_specs=[SMEM, HBM, VMEM],
        out_specs=[VMEM] * inner,
        out_shape=[
            jax.ShapeDtypeStruct((count // inner, rows, width), jnp.bfloat16 if dx else jnp.float32)
            for dx in range(inner)
        ],
        scratch_shapes=[
            pltpu.VMEM((count, depth, width), weights.dtype),
            pltpu.SemaphoreType.DMA((count,)),
        ],
        compiler_params=params(14),
        name="partials",
    )(at, in_hbm(weights), inputs)


def added(at, among, own, arrived):
    count, rows, width = own.shape

    def body(at, own_ref, *refs):
        arrived_refs, out_refs = refs[: len(arrived)], refs[len(arrived) :]

        @pl.when((at[0] >= min(among)) & (at[0] <= max(among)))
        def _():
            for n in range(count):
                total = own_ref[n]
                for ref in arrived_refs:
                    total = total + ref[n].astype(jnp.float32)
                out_refs[n][...] = total.astype(out_refs[n].dtype)

    return pl.pallas_call(
        body,
        in_specs=[SMEM] + [VMEM] * (1 + len(arrived)),
        out_specs=[VMEM] * count,
        out_shape=[
            jax.ShapeDtypeStruct((rows, width), jnp.bfloat16 if n else jnp.float32)
            for n in range(count)
        ],
        compiler_params=params(4),
        name="added",
    )(at, own, *arrived)


def mean_square(at, half, rot_outs, low, high, low_runs, high_runs, micro, seq):
    _, rows, width = low[0].shape
    eig_rows = rot_outs[0].shape[1]
    count, sections = len(low_runs), len(rot_outs)

    def body(at, *refs):
        rot_refs, refs = refs[:sections], refs[sections:]
        low_refs, refs = refs[: len(low)], refs[len(low) :]
        high_refs, refs = refs[: len(high)], refs[len(high) :]
        eig_ref, rot, block, result, sems = refs
        for s in range(sections):

            @pl.when(at[0] == s)
            def _():
                rot[...] = rot_refs[s][...]

        def copy(n):
            return pltpu.make_async_copy(
                result.at[n % 2], run_of(eig_ref, 1, at[1 + n], width), sems.at[n % 2]
            )

        for n in range(count):

            @pl.when(at[0] >= half)
            def _():
                a, i = high_runs[n]
                block[...] = high_refs[a][i]

            @pl.when(at[0] < half)
            def _():
                a, i = low_runs[n]
                block[...] = low_refs[a][i]

            if n >= 2:
                copy(n - 2).wait()
            for m in range(micro):
                rows_of = slice(m * seq, (m + 1) * seq)
                product = lax.dot_general(
                    rot[rows_of, :],
                    block[rows_of, :],
                    (((0,), (0,)), ((), ())),
                    preferred_element_type=jnp.float32,
                )
                square = product * product
                total = square if m == 0 else result[n % 2] + square
                result[n % 2] = total if m < micro - 1 else total * (1.0 / (seq * micro))
            copy(n).start()
        for n in range(max(0, count - 2), count):
            copy(n).wait()

    return pl.pallas_call(
        body,
        in_specs=[SMEM] + [VMEM] * (sections + len(low) + len(high)),
        out_specs=HBM,
        out_shape=jax.ShapeDtypeStruct((eig_rows, count * width), jnp.float32),
        scratch_shapes=[
            pltpu.VMEM((rows, eig_rows), rot_outs[0].dtype),
            pltpu.VMEM((rows, width), rot_outs[0].dtype),
            pltpu.VMEM((2, eig_rows, width), jnp.float32),
            pltpu.SemaphoreType.DMA((2,)),
        ],
        compiler_params=params(14),
        name="mean_square",
    )(at, *rot_outs, *low, *high)


def per_device(activations, top_grad, projection, basis_out, basis_in):
    sections = lax.axis_size("section")
    shards = lax.axis_size("shard")
    micro, seq, feat_loc = top_grad.shape
    rows = micro * seq
    inputs = activations[0].reshape(rows, feat_loc)
    top = top_grad.reshape(rows, feat_loc)
    weights, out_cols = projection[0], basis_out[0]
    half = sections // 2

    inner = 1
    while 2 * (2 * inner) ** 2 <= shards:
        inner *= 2
    outer = shards // inner
    shard = lax.axis_index("shard")
    at = jnp.stack(
        [jnp.int32(lax.axis_index("section"))] + [jnp.int32(shard ^ p) for p in range(shards)]
    )

    def moved(block, flip, pairs):
        route = [(a * shards + i, b * shards + (i ^ flip)) for a, b in pairs for i in range(shards)]
        return lax.ppermute(block, ("section", "shard"), route)

    def spread(block, pairs):
        powers = [1 << p for p in range(outer.bit_length() - 1)]
        near = {dz: moved(block, dz * inner, pairs) for dz in reversed(powers)}
        return near, {dx: moved(block, dx, pairs) for dx in range(1, inner)}

    def along_outer(near, pairs, after=()):
        got = dict(near)
        for dz in range(outer):
            low = dz & -dz
            if dz not in got:
                block, *_ = lax.optimization_barrier((got[dz ^ low], *after))
                got[dz] = moved(block, low * inner, pairs)
        return got

    def handed_down(grad, turn, after=()):
        own = moved(grad, 0, [(turn + 1, turn)])
        if turn % 2 == 0:
            near, side = spread(grad, [(turn + 1, turn)])
        else:
            own, *_ = lax.optimization_barrier((own, *after))
            near, side = spread(own, [(turn, turn)])
        return {0: own, **near}, side

    order = [0] + [1 << p for p in reversed(range(outer.bit_length() - 1))]
    order += [dz for dz in range(outer) if dz not in order]

    def relay(turn, sent, before, within, matrix):
        near, side = sent
        got = along_outer(near, [(turn, turn)])
        start, *_ = lax.optimization_barrier((near[0], *before))

        def products(dots, base, last):
            blocks, parts = [block for block, _ in dots], [part for _, part in dots]
            out_type = jnp.bfloat16 if last else jnp.float32
            return block_dot(at, turn, blocks, matrix, parts, base, out_type)

        blocks = {(0, 0): start, **{(0, dx): block for dx, block in side.items()}}
        dots = [(block, dx) for (_, dx), block in blocks.items()]
        totals = [products(dots, None if turn == 0 else start, outer == 1)]
        for n in range(1, outer + 1):
            if n < outer:
                dz = order[n]
                ties = [totals[0] if n > 1 or turn < sections - 1 else matrix]
                ties += [blocks[order[max(0, n - 2)], dx] for dx in range(1, inner)]
                block, *_ = lax.optimization_barrier(
                    (got[dz], *ties, *(within if n == outer - 1 else []))
                )
                blocks[dz, 0] = got[dz]
                for dx in range(1, inner):
                    blocks[dz, dx] = moved(block, dx, [(turn, turn)])
            if n > 1:
                dz = order[n - 1]
                dots = [(blocks[dz, dx], dz * inner + dx) for dx in range(inner)]
                if n == outer - 1:
                    dots.append((blocks[order[n], 0], order[n] * inner))
                if n == outer and outer > 2 and inner > 1:
                    dots = dots[1:]
                totals.append(products(dots, totals[-1], n == outer))
        return totals[-1], blocks

    def rotated(turn, blocks):
        parts = [dz * inner + dx for dz, dx in blocks]
        return stream_dot(at, turn, list(blocks.values()), out_cols, parts, jnp.bfloat16)

    def rotate_begin(inputs, among):
        pairs = [(a, a) for a in among]
        own, *others = partials(at, among, inputs, basis_in[0], inner)
        return own, others, [moved(other, 1 + n, pairs) for n, other in enumerate(others)]

    def summed(sums, among):
        pairs = [(a, a) for a in among]
        own = sums[0]
        for dz, part in enumerate(sums[1:], 1):
            own = own + moved(part, dz * inner, pairs).astype(jnp.float32)
        return own.astype(jnp.bfloat16)

    def outer_columns(own, among, halves, after=()):
        pairs = [(a, a) for a in among]
        powers = [1 << p for p in range(outer.bit_length() - 1)]
        near = {0: own, **{dz: moved(own, dz * inner, pairs) for dz in reversed(powers)}}
        got = along_outer(near, pairs, after)
        return [jnp.stack([got[dz] for dz in some]) for some in halves]

    def all_columns(columns, among):
        pairs = [(a, a) for a in among]
        return [[c] + [moved(c, dx, pairs) for dx in range(1, inner)] for c in columns]

    upper = list(range(sections - 1, half - 1, -1))
    lower = list(range(half - 1, -1, -1))
    rot_outs = [None] * sections

    low_own, low_others, low_arrived = rotate_begin(inputs, lower)
    near, side = spread(top, [(upper[0], upper[0])])
    weights = resident(at, weights)
    halves = [order]
    sums = added(at, lower, low_own, low_arrived)
    low = summed(sums, lower)
    sent, before, within = ({0: top, **near}, side), low_others, sums
    for turn in upper:
        grad, blocks = relay(turn, sent, before, within, weights)
        if turn != upper[-1]:
            sent = handed_down(grad, turn - 1)
            rot_outs[turn] = rotated(turn, blocks)
            before, within = [low], [rot_outs[turn]]
    low = outer_columns(low, lower, halves, [grad])
    sent = handed_down(grad, lower[0], low)
    low = all_columns(low, lower)
    rot_outs[upper[-1]] = rotated(upper[-1], blocks)
    inputs, *_ = lax.optimization_barrier((inputs, sent[0][0]))
    last_cols = resident(at, out_cols, 0)
    high_own, _, high_arrived = rotate_begin(inputs, upper)
    before, within = [], [rot_outs[upper[-1]], *jax.tree.leaves(low)]
    for turn in lower:
        grad, blocks = relay(turn, sent, before, within, weights if turn else last_cols)
        if turn != 0:
            sent = handed_down(grad, turn - 1)
            rot_outs[turn] = rotated(turn, blocks)
            before, within = [], [rot_outs[turn]]
    rot_outs[0] = grad
    sums = added(at, upper, high_own, high_arrived)
    high = all_columns(outer_columns(summed(sums, upper), upper, [order]), upper)

    def runs(parts):
        place = {dz: (a, i) for a, some in enumerate(parts) for i, dz in enumerate(some)}
        return [(place[p // inner][0] * inner + p % inner, place[p // inner][1]) for p in range(shards)]

    low, high = jax.tree.leaves(low), jax.tree.leaves(high)
    return mean_square(
        at, half, rot_outs, low, high, runs(halves), runs([order]), micro, seq
    )[None]


def solution(mesh):
    return jax.shard_map(
        per_device,
        mesh=mesh,
        in_specs=(
            P("section", None, None, "shard"),
            P(None, None, "shard"),
            P("section", None, "shard"),
            P("section", None, "shard"),
            P("section", "shard", None),
        ),
        out_specs=P("section", "shard", None),
        check_vma=False,
    )
```

```python
import jax
import jax.numpy as jnp
from jax import lax
from jax.experimental import pallas as pl
from jax.experimental.pallas import tpu as pltpu
from jax.sharding import PartitionSpec as P

VMEM = pl.BlockSpec(memory_space=pltpu.VMEM)
SMEM = pl.BlockSpec(memory_space=pltpu.SMEM)
HBM = pl.BlockSpec(memory_space=pltpu.HBM)


def params(megabytes):
    return pltpu.CompilerParams(vmem_limit_bytes=megabytes * 1024 * 1024)


def in_hbm(array):
    return pltpu.with_memory_space_constraint(array, pltpu.HBM)


def run_of(ref, axis, at, length):
    part = pl.ds(pl.multiple_of(at * length, length), length)
    return ref.at[part, :] if axis == 0 else ref.at[:, part]


def resident(at, weights, only=None):
    count = at.shape[0] - 1
    depth, cols = weights.shape[0] // count, weights.shape[1]

    def body(at, weights_ref, out_ref, sems):
        def copy(i):
            return pltpu.make_async_copy(
                run_of(weights_ref, 0, at[1 + i], depth), out_ref.at[i], sems.at[i]
            )

        @pl.when((at[0] == only) if only is not None else (at[0] >= 0))
        def _():
            for i in range(count):
                copy(i).start()
            for i in range(count):
                copy(i).wait()

    return pl.pallas_call(
        body,
        in_specs=[SMEM, HBM],
        out_specs=VMEM,
        out_shape=jax.ShapeDtypeStruct((count, depth, cols), weights.dtype),
        scratch_shapes=[pltpu.SemaphoreType.DMA((count,))],
        compiler_params=params(4),
        name="resident",
    )(at, in_hbm(weights))


def block_dot(at, turn, blocks, weights, parts, base, out_type):
    rows, depth = blocks[0].shape
    cols = weights.shape[2]
    width = 256 if cols % 256 == 0 else cols
    count = len(blocks)

    def body(at, weights_ref, *refs):
        @pl.when(at[0] == turn)
        def _():
            def tile(j, _):
                here = pl.ds(pl.multiple_of(j * width, width), width)
                total = None if base is None else refs[count][:, here].astype(jnp.float32)
                for block_ref, part in zip(refs[:count], parts):
                    product = jnp.dot(
                        block_ref[...],
                        weights_ref[part, :, here],
                        preferred_element_type=jnp.float32,
                    )
                    total = product if total is None else total + product
                refs[-1][:, here] = total.astype(out_type)
                return 0

            lax.fori_loop(0, cols // width, tile, 0)

    return pl.pallas_call(
        body,
        in_specs=[SMEM] + [VMEM] * (1 + count + (base is not None)),
        out_specs=VMEM,
        out_shape=jax.ShapeDtypeStruct((rows, cols), out_type),
        compiler_params=params(4),
        name="block_dot",
    )(at, weights, *blocks, *([] if base is None else [base]))


def stream_dot(at, turn, blocks, weights, parts, out_type):
    rows, depth = blocks[0].shape
    cols = weights.shape[1]
    count = len(blocks)

    def body(at, weights_ref, *refs):
        block_refs, (out_ref, runs, sems) = refs[:count], refs[-3:]

        def copy(k):
            return pltpu.make_async_copy(
                run_of(weights_ref, 0, at[1 + parts[k]], depth), runs.at[k], sems.at[k]
            )

        @pl.when(at[0] == turn)
        def _():
            for k in range(count):
                copy(k).start()
            total = None
            for k in range(count):
                copy(k).wait()
                part = jnp.dot(block_refs[k][...], runs[k], preferred_element_type=jnp.float32)
                total = part if total is None else total + part
            out_ref[...] = total.astype(out_type)

    return pl.pallas_call(
        body,
        in_specs=[SMEM, HBM] + [VMEM] * count,
        out_specs=VMEM,
        out_shape=jax.ShapeDtypeStruct((rows, cols), out_type),
        scratch_shapes=[
            pltpu.VMEM((count, depth, cols), weights.dtype),
            pltpu.SemaphoreType.DMA((count,)),
        ],
        compiler_params=params(14),
        name="stream_dot",
    )(at, in_hbm(weights), *blocks)


def partials(at, among, inputs, weights, inner):
    rows, depth = inputs.shape
    count = at.shape[0] - 1
    width = weights.shape[1] // count

    def body(at, weights_ref, inputs_ref, *refs):
        out_refs, (runs, sems) = refs[:inner], refs[inner:]
        order = [n for dx in [*range(1, inner), 0] for n in range(dx, count, inner)]

        def copy(n):
            return pltpu.make_async_copy(
                run_of(weights_ref, 1, at[1 + n], width), runs.at[n], sems.at[n]
            )

        @pl.when((at[0] >= min(among)) & (at[0] <= max(among)))
        def _():
            for n in order:
                copy(n).start()
            for n in order:
                copy(n).wait()
                total = jnp.dot(inputs_ref[...], runs[n], preferred_element_type=jnp.float32)
                out_ref = out_refs[n % inner]
                out_ref[n // inner] = total.astype(out_ref.dtype)

    return pl.pallas_call(
        body,
        in_specs=[SMEM, HBM, VMEM],
        out_specs=[VMEM] * inner,
        out_shape=[
            jax.ShapeDtypeStruct((count // inner, rows, width), jnp.bfloat16 if dx else jnp.float32)
            for dx in range(inner)
        ],
        scratch_shapes=[
            pltpu.VMEM((count, depth, width), weights.dtype),
            pltpu.SemaphoreType.DMA((count,)),
        ],
        compiler_params=params(14),
        name="partials",
    )(at, in_hbm(weights), inputs)


def added(at, among, own, arrived, old=()):
    count, rows, width = own.shape

    def body(at, own_ref, *refs):
        arrived_refs, out_refs = refs[: len(arrived)], refs[len(arrived) + len(old) :]

        @pl.when((at[0] >= min(among)) & (at[0] <= max(among)))
        def _():
            for n in range(count):
                total = own_ref[n]
                for ref in arrived_refs:
                    total = total + ref[n].astype(jnp.float32)
                out_refs[n][...] = total.astype(out_refs[n].dtype)

    return pl.pallas_call(
        body,
        in_specs=[SMEM] + [VMEM] * (1 + len(arrived) + len(old)),
        input_output_aliases={2 + len(arrived) + n: n for n in range(len(old))},
        out_specs=[VMEM] * count,
        out_shape=[
            jax.ShapeDtypeStruct((rows, width), jnp.bfloat16 if n else jnp.float32)
            for n in range(count)
        ],
        compiler_params=params(4),
        name="added",
    )(at, own, *arrived, *old)


def mean_square(at, half, rot_outs, low, high, low_runs, high_runs, micro, seq):
    _, rows, width = low[0].shape
    eig_rows = rot_outs[0].shape[1]
    count, sections = len(low_runs), len(rot_outs)

    def body(at, *refs):
        rot_refs, refs = refs[:sections], refs[sections:]
        low_refs, refs = refs[: len(low)], refs[len(low) :]
        high_refs, refs = refs[: len(high)], refs[len(high) :]
        eig_ref, rot, block, result, sems = refs
        for s in range(sections):

            @pl.when(at[0] == s)
            def _():
                rot[...] = rot_refs[s][...]

        def copy(n):
            return pltpu.make_async_copy(
                result.at[n % 2], run_of(eig_ref, 1, at[1 + n], width), sems.at[n % 2]
            )

        for n in range(count):

            @pl.when(at[0] >= half)
            def _():
                a, i = high_runs[n]
                block[...] = high_refs[a][i]

            @pl.when(at[0] < half)
            def _():
                a, i = low_runs[n]
                block[...] = low_refs[a][i]

            if n >= 2:
                copy(n - 2).wait()
            for m in range(micro):
                rows_of = slice(m * seq, (m + 1) * seq)
                product = lax.dot_general(
                    rot[rows_of, :],
                    block[rows_of, :],
                    (((0,), (0,)), ((), ())),
                    preferred_element_type=jnp.float32,
                )
                square = product * product
                total = square if m == 0 else result[n % 2] + square
                result[n % 2] = total if m < micro - 1 else total * (1.0 / (seq * micro))
            copy(n).start()
        for n in range(max(0, count - 2), count):
            copy(n).wait()

    return pl.pallas_call(
        body,
        in_specs=[SMEM] + [VMEM] * (sections + len(low) + len(high)),
        out_specs=HBM,
        out_shape=jax.ShapeDtypeStruct((eig_rows, count * width), jnp.float32),
        scratch_shapes=[
            pltpu.VMEM((rows, eig_rows), rot_outs[0].dtype),
            pltpu.VMEM((rows, width), rot_outs[0].dtype),
            pltpu.VMEM((2, eig_rows, width), jnp.float32),
            pltpu.SemaphoreType.DMA((2,)),
        ],
        compiler_params=params(14),
        name="mean_square",
    )(at, *rot_outs, *low, *high)


def per_device(activations, top_grad, projection, basis_out, basis_in):
    sections = lax.axis_size("section")
    shards = lax.axis_size("shard")
    micro, seq, feat_loc = top_grad.shape
    rows = micro * seq
    inputs = activations[0].reshape(rows, feat_loc)
    top = top_grad.reshape(rows, feat_loc)
    weights, out_cols = projection[0], basis_out[0]
    half = sections // 2

    inner = 1
    while 2 * (2 * inner) ** 2 <= shards:
        inner *= 2
    outer = shards // inner
    shard = lax.axis_index("shard")
    at = jnp.stack(
        [jnp.int32(lax.axis_index("section"))] + [jnp.int32(shard ^ p) for p in range(shards)]
    )

    def moved(block, flip, pairs):
        route = [(a * shards + i, b * shards + (i ^ flip)) for a, b in pairs for i in range(shards)]
        return lax.ppermute(block, ("section", "shard"), route)

    def spread(block, pairs):
        powers = [1 << p for p in range(outer.bit_length() - 1)]
        near = {dz: moved(block, dz * inner, pairs) for dz in reversed(powers)}
        return near, {dx: moved(block, dx, pairs) for dx in range(1, inner)}

    def along_outer(near, pairs, after=()):
        got = dict(near)
        for dz in range(outer):
            low = dz & -dz
            if dz not in got:
                block, *_ = lax.optimization_barrier((got[dz ^ low], *after))
                got[dz] = moved(block, low * inner, pairs)
        return got

    def handed_down(grad, turn, after=()):
        own = moved(grad, 0, [(turn + 1, turn)])
        if turn % 2 == 0:
            near, side = spread(grad, [(turn + 1, turn)])
        else:
            own, *_ = lax.optimization_barrier((own, *after))
            near, side = spread(own, [(turn, turn)])
        return {0: own, **near}, side

    order = [0] + [1 << p for p in reversed(range(outer.bit_length() - 1))]
    order += [dz for dz in range(outer) if dz not in order]

    def relay(turn, sent, before, within, matrix):
        near, side = sent
        got = along_outer(near, [(turn, turn)])
        start, *_ = lax.optimization_barrier((near[0], *before))

        def products(dots, base, last):
            blocks, parts = [block for block, _ in dots], [part for _, part in dots]
            out_type = jnp.bfloat16 if last else jnp.float32
            return block_dot(at, turn, blocks, matrix, parts, base, out_type)

        blocks = {(0, 0): start, **{(0, dx): block for dx, block in side.items()}}
        dots = [(block, dx) for (_, dx), block in blocks.items()]
        totals = [products(dots, None if turn == 0 else start, outer == 1)]
        for n in range(1, outer + 1):
            if n < outer:
                dz = order[n]
                ties = [totals[0] if n > 1 or turn < sections - 1 else matrix]
                ties += [blocks[order[max(0, n - 2)], dx] for dx in range(1, inner)]
                block, *_ = lax.optimization_barrier(
                    (got[dz], *ties, *(within if n == outer - 1 else []))
                )
                blocks[dz, 0] = got[dz]
                for dx in range(1, inner):
                    blocks[dz, dx] = moved(block, dx, [(turn, turn)])
            if n > 1:
                dz = order[n - 1]
                dots = [(blocks[dz, dx], dz * inner + dx) for dx in range(inner)]
                if n == outer - 1:
                    dots.append((blocks[order[n], 0], order[n] * inner))
                if n == outer and outer > 2 and inner > 1:
                    dots = dots[1:]
                totals.append(products(dots, totals[-1], n == outer))
        return totals[-1], blocks

    def rotated(turn, blocks):
        parts = [dz * inner + dx for dz, dx in blocks]
        return stream_dot(at, turn, list(blocks.values()), out_cols, parts, jnp.bfloat16)

    def rotate_begin(inputs, among):
        pairs = [(a, a) for a in among]
        own, *others = partials(at, among, inputs, basis_in[0], inner)
        return own, others, [moved(other, 1 + n, pairs) for n, other in enumerate(others)]

    def summed(sums, among):
        pairs = [(a, a) for a in among]
        own = sums[0]
        for dz, part in enumerate(sums[1:], 1):
            own = own + moved(part, dz * inner, pairs).astype(jnp.float32)
        return own.astype(jnp.bfloat16)

    def outer_columns(own, among, halves, after=()):
        pairs = [(a, a) for a in among]
        powers = [1 << p for p in range(outer.bit_length() - 1)]
        near = {0: own, **{dz: moved(own, dz * inner, pairs) for dz in reversed(powers)}}
        got = along_outer(near, pairs, after)
        return [jnp.stack([got[dz] for dz in some]) for some in halves]

    def all_columns(columns, among):
        pairs = [(a, a) for a in among]
        return [[c] + [moved(c, dx, pairs) for dx in range(1, inner)] for c in columns]

    upper = list(range(sections - 1, half - 1, -1))
    lower = list(range(half - 1, -1, -1))
    rot_outs = [None] * sections

    first = lower + upper[1:]
    own, others, arrived = rotate_begin(inputs, first)
    near, side = spread(top, [(upper[0], upper[0])])
    weights = resident(at, weights)
    halves = [order]
    sums = added(at, lower, own, arrived)
    low = summed(sums, lower)
    sent, before, within = ({0: top, **near}, side), others, sums
    for turn in upper:
        grad, blocks = relay(turn, sent, before, within, weights)
        if turn != upper[-1]:
            sent = handed_down(grad, turn - 1)
            rot_outs[turn] = rotated(turn, blocks)
            before, within = [low], [rot_outs[turn]]
        if turn == upper[0]:
            inputs, _ = lax.optimization_barrier((inputs, grad))
            last_own, last_others, last_arrived = rotate_begin(inputs, upper[:1])
            before, within = before + last_others, within + last_arrived
    low = outer_columns(low, lower, halves, [grad])
    sent = handed_down(grad, lower[0], low)
    low = all_columns(low, lower)
    rot_outs[upper[-1]] = rotated(upper[-1], blocks)
    last_cols = resident(at, out_cols, 0)
    own, last_own, _ = lax.optimization_barrier((own, last_own, sent[0][0]))
    before, within = [], [rot_outs[upper[-1]], *jax.tree.leaves(low)]
    for turn in lower:
        grad, blocks = relay(turn, sent, before, within, weights if turn else last_cols)
        if turn != 0:
            sent = handed_down(grad, turn - 1)
            rot_outs[turn] = rotated(turn, blocks)
            before, within = [], [rot_outs[turn]]
    rot_outs[0] = grad
    sums = added(at, upper[:1], last_own, last_arrived, added(at, upper[1:], own, arrived))
    high = all_columns(outer_columns(summed(sums, upper), upper, [order]), upper)

    def runs(parts):
        place = {dz: (a, i) for a, some in enumerate(parts) for i, dz in enumerate(some)}
        return [(place[p // inner][0] * inner + p % inner, place[p // inner][1]) for p in range(shards)]

    low, high = jax.tree.leaves(low), jax.tree.leaves(high)
    return mean_square(
        at, half, rot_outs, low, high, runs(halves), runs([order]), micro, seq
    )[None]


def solution(mesh):
    return jax.shard_map(
        per_device,
        mesh=mesh,
        in_specs=(
            P("section", None, None, "shard"),
            P(None, None, "shard"),
            P("section", None, "shard"),
            P("section", None, "shard"),
            P("section", "shard", None),
        ),
        out_specs=P("section", "shard", None),
        check_vma=False,
    )
```

```python
import jax
import jax.numpy as jnp
from jax import lax
from jax.experimental import pallas as pl
from jax.experimental.pallas import tpu as pltpu
from jax.sharding import PartitionSpec as P

VMEM = pl.BlockSpec(memory_space=pltpu.VMEM)
SMEM = pl.BlockSpec(memory_space=pltpu.SMEM)
HBM = pl.BlockSpec(memory_space=pltpu.HBM)


def params(megabytes):
    return pltpu.CompilerParams(vmem_limit_bytes=megabytes * 1024 * 1024)


def in_hbm(array):
    return pltpu.with_memory_space_constraint(array, pltpu.HBM)


def run_of(ref, axis, at, length):
    part = pl.ds(pl.multiple_of(at * length, length), length)
    return ref.at[part, :] if axis == 0 else ref.at[:, part]


def resident(at, weights, only=None):
    count = at.shape[0] - 1
    depth, cols = weights.shape[0] // count, weights.shape[1]

    def body(at, weights_ref, out_ref, sems):
        def copy(i):
            return pltpu.make_async_copy(
                run_of(weights_ref, 0, at[1 + i], depth), out_ref.at[i], sems.at[i]
            )

        @pl.when((at[0] == only) if only is not None else (at[0] >= 0))
        def _():
            for i in range(count):
                copy(i).start()
            for i in range(count):
                copy(i).wait()

    return pl.pallas_call(
        body,
        in_specs=[SMEM, HBM],
        out_specs=VMEM,
        out_shape=jax.ShapeDtypeStruct((count, depth, cols), weights.dtype),
        scratch_shapes=[pltpu.SemaphoreType.DMA((count,))],
        compiler_params=params(4),
        name="resident",
    )(at, in_hbm(weights))


def block_dot(at, turn, blocks, weights, parts, base, out_type):
    rows, depth = blocks[0].shape
    cols = weights.shape[2]
    width = 256 if cols % 256 == 0 else cols
    count = len(blocks)

    def body(at, weights_ref, *refs):
        @pl.when(at[0] == turn)
        def _():
            def tile(j, _):
                here = pl.ds(pl.multiple_of(j * width, width), width)
                total = None if base is None else refs[count][:, here].astype(jnp.float32)
                for block_ref, part in zip(refs[:count], parts):
                    product = jnp.dot(
                        block_ref[...],
                        weights_ref[part, :, here],
                        preferred_element_type=jnp.float32,
                    )
                    total = product if total is None else total + product
                refs[-1][:, here] = total.astype(out_type)
                return 0

            lax.fori_loop(0, cols // width, tile, 0)

    return pl.pallas_call(
        body,
        in_specs=[SMEM] + [VMEM] * (1 + count + (base is not None)),
        out_specs=VMEM,
        out_shape=jax.ShapeDtypeStruct((rows, cols), out_type),
        compiler_params=params(4),
        name="block_dot",
    )(at, weights, *blocks, *([] if base is None else [base]))


def stream_dot(at, turn, blocks, weights, parts, out_type):
    rows, depth = blocks[0].shape
    cols = weights.shape[1]
    count = len(blocks)

    def body(at, weights_ref, *refs):
        block_refs, (out_ref, runs, sems) = refs[:count], refs[-3:]

        def copy(k):
            return pltpu.make_async_copy(
                run_of(weights_ref, 0, at[1 + parts[k]], depth), runs.at[k], sems.at[k]
            )

        @pl.when(at[0] == turn)
        def _():
            for k in range(count):
                copy(k).start()
            total = None
            for k in range(count):
                copy(k).wait()
                part = jnp.dot(block_refs[k][...], runs[k], preferred_element_type=jnp.float32)
                total = part if total is None else total + part
            out_ref[...] = total.astype(out_type)

    return pl.pallas_call(
        body,
        in_specs=[SMEM, HBM] + [VMEM] * count,
        out_specs=VMEM,
        out_shape=jax.ShapeDtypeStruct((rows, cols), out_type),
        scratch_shapes=[
            pltpu.VMEM((count, depth, cols), weights.dtype),
            pltpu.SemaphoreType.DMA((count,)),
        ],
        compiler_params=params(14),
        name="stream_dot",
    )(at, in_hbm(weights), *blocks)


def partials(at, among, inputs, weights, inner):
    rows, depth = inputs.shape
    count = at.shape[0] - 1
    width = weights.shape[1] // count

    def body(at, weights_ref, inputs_ref, *refs):
        out_refs, (runs, sems) = refs[:inner], refs[inner:]
        order = [n for dx in [*range(1, inner), 0] for n in range(dx, count, inner)]

        def copy(n):
            return pltpu.make_async_copy(
                run_of(weights_ref, 1, at[1 + n], width), runs.at[n], sems.at[n]
            )

        @pl.when((at[0] >= min(among)) & (at[0] <= max(among)))
        def _():
            for n in order:
                copy(n).start()
            for n in order:
                copy(n).wait()
                total = jnp.dot(inputs_ref[...], runs[n], preferred_element_type=jnp.float32)
                out_ref = out_refs[n % inner]
                out_ref[n // inner] = total.astype(out_ref.dtype)

    return pl.pallas_call(
        body,
        in_specs=[SMEM, HBM, VMEM],
        out_specs=[VMEM] * inner,
        out_shape=[
            jax.ShapeDtypeStruct((count // inner, rows, width), jnp.bfloat16 if dx else jnp.float32)
            for dx in range(inner)
        ],
        scratch_shapes=[
            pltpu.VMEM((count, depth, width), weights.dtype),
            pltpu.SemaphoreType.DMA((count,)),
        ],
        compiler_params=params(14),
        name="partials",
    )(at, in_hbm(weights), inputs)


def added(at, among, own, arrived, old=()):
    count, rows, width = own.shape

    def body(at, own_ref, *refs):
        arrived_refs, out_refs = refs[: len(arrived)], refs[len(arrived) + len(old) :]

        @pl.when((at[0] >= min(among)) & (at[0] <= max(among)))
        def _():
            for n in range(count):
                total = own_ref[n]
                for ref in arrived_refs:
                    total = total + ref[n].astype(jnp.float32)
                out_refs[n][...] = total.astype(out_refs[n].dtype)

    return pl.pallas_call(
        body,
        in_specs=[SMEM] + [VMEM] * (1 + len(arrived) + len(old)),
        input_output_aliases={2 + len(arrived) + n: n for n in range(len(old))},
        out_specs=[VMEM] * count,
        out_shape=[
            jax.ShapeDtypeStruct((rows, width), jnp.bfloat16 if n else jnp.float32)
            for n in range(count)
        ],
        compiler_params=params(4),
        name="added",
    )(at, own, *arrived, *old)


def mean_square(at, half, rot_outs, low, high, low_runs, high_runs, micro, seq):
    _, rows, width = low[0].shape
    eig_rows = rot_outs[0].shape[1]
    count, sections = len(low_runs), len(rot_outs)

    def body(at, *refs):
        rot_refs, refs = refs[:sections], refs[sections:]
        low_refs, refs = refs[: len(low)], refs[len(low) :]
        high_refs, refs = refs[: len(high)], refs[len(high) :]
        eig_ref, rot, block, result, sems = refs
        for s in range(sections):

            @pl.when(at[0] == s)
            def _():
                rot[...] = rot_refs[s][...]

        def copy(n):
            return pltpu.make_async_copy(
                result.at[n % 2], run_of(eig_ref, 1, at[1 + n], width), sems.at[n % 2]
            )

        for n in range(count):

            @pl.when(at[0] >= half)
            def _():
                a, i = high_runs[n]
                block[...] = high_refs[a][i]

            @pl.when(at[0] < half)
            def _():
                a, i = low_runs[n]
                block[...] = low_refs[a][i]

            if n >= 2:
                copy(n - 2).wait()
            for m in range(micro):
                rows_of = slice(m * seq, (m + 1) * seq)
                product = lax.dot_general(
                    rot[rows_of, :],
                    block[rows_of, :],
                    (((0,), (0,)), ((), ())),
                    preferred_element_type=jnp.float32,
                )
                square = product * product
                total = square if m == 0 else result[n % 2] + square
                result[n % 2] = total if m < micro - 1 else total * (1.0 / (seq * micro))
            copy(n).start()
        for n in range(max(0, count - 2), count):
            copy(n).wait()

    return pl.pallas_call(
        body,
        in_specs=[SMEM] + [VMEM] * (sections + len(low) + len(high)),
        out_specs=HBM,
        out_shape=jax.ShapeDtypeStruct((eig_rows, count * width), jnp.float32),
        scratch_shapes=[
            pltpu.VMEM((rows, eig_rows), rot_outs[0].dtype),
            pltpu.VMEM((rows, width), rot_outs[0].dtype),
            pltpu.VMEM((2, eig_rows, width), jnp.float32),
            pltpu.SemaphoreType.DMA((2,)),
        ],
        compiler_params=params(14),
        name="mean_square",
    )(at, *rot_outs, *low, *high)


def per_device(activations, top_grad, projection, basis_out, basis_in):
    sections = lax.axis_size("section")
    shards = lax.axis_size("shard")
    micro, seq, feat_loc = top_grad.shape
    rows = micro * seq
    inputs = activations[0].reshape(rows, feat_loc)
    top = top_grad.reshape(rows, feat_loc)
    weights, out_cols = projection[0], basis_out[0]
    half = sections // 2

    inner = 1
    while 2 * (2 * inner) ** 2 <= shards:
        inner *= 2
    outer = shards // inner
    shard = lax.axis_index("shard")
    at = jnp.stack(
        [jnp.int32(lax.axis_index("section"))] + [jnp.int32(shard ^ p) for p in range(shards)]
    )

    def moved(block, flip, pairs):
        route = [(a * shards + i, b * shards + (i ^ flip)) for a, b in pairs for i in range(shards)]
        return lax.ppermute(block, ("section", "shard"), route)

    def spread(block, pairs):
        powers = [1 << p for p in range(outer.bit_length() - 1)]
        near = {dz: moved(block, dz * inner, pairs) for dz in reversed(powers)}
        return near, {dx: moved(block, dx, pairs) for dx in range(1, inner)}

    def along_outer(near, pairs, after=()):
        got = dict(near)
        for dz in range(outer):
            low = dz & -dz
            if dz not in got:
                block, *_ = lax.optimization_barrier((got[dz ^ low], *after))
                got[dz] = moved(block, low * inner, pairs)
        return got

    def handed_down(grad, turn, after=()):
        own = moved(grad, 0, [(turn + 1, turn)])
        if turn % 2 == 0:
            near, side = spread(grad, [(turn + 1, turn)])
        else:
            own, *_ = lax.optimization_barrier((own, *after))
            near, side = spread(own, [(turn, turn)])
        return {0: own, **near}, side

    order = [0] + [1 << p for p in reversed(range(outer.bit_length() - 1))]
    order += [dz for dz in range(outer) if dz not in order]

    def relay(turn, sent, before, within, matrix):
        near, side = sent
        got = along_outer(near, [(turn, turn)])
        start, *_ = lax.optimization_barrier((near[0], *before))

        def products(dots, base, last):
            blocks, parts = [block for block, _ in dots], [part for _, part in dots]
            out_type = jnp.bfloat16 if last else jnp.float32
            return block_dot(at, turn, blocks, matrix, parts, base, out_type)

        blocks = {(0, 0): start, **{(0, dx): block for dx, block in side.items()}}
        dots = [(block, dx) for (_, dx), block in blocks.items()]
        totals = [products(dots, None if turn == 0 else start, outer == 1)]
        for n in range(1, outer + 1):
            if n < outer:
                dz = order[n]
                ties = [totals[0] if n > 1 or turn < sections - 1 else matrix]
                ties += [blocks[order[max(0, n - 2)], dx] for dx in range(1, inner)]
                block, *_ = lax.optimization_barrier(
                    (got[dz], *ties, *(within if n == outer - 1 else []))
                )
                blocks[dz, 0] = got[dz]
                for dx in range(1, inner):
                    blocks[dz, dx] = moved(block, dx, [(turn, turn)])
            if n > 1:
                dz = order[n - 1]
                dots = [(blocks[dz, dx], dz * inner + dx) for dx in range(inner)]
                if n == outer - 1:
                    dots.append((blocks[order[n], 0], order[n] * inner))
                if n == outer and outer > 2 and inner > 1:
                    dots = dots[1:]
                totals.append(products(dots, totals[-1], n == outer))
        return totals[-1], blocks

    def rotated(turn, blocks):
        parts = [dz * inner + dx for dz, dx in blocks]
        return stream_dot(at, turn, list(blocks.values()), out_cols, parts, jnp.bfloat16)

    def rotate_begin(inputs, among):
        pairs = [(a, a) for a in among]
        own, *others = partials(at, among, inputs, basis_in[0], inner)
        return own, others, [moved(other, 1 + n, pairs) for n, other in enumerate(others)]

    def summed(sums, among):
        pairs = [(a, a) for a in among]
        own = sums[0]
        for dz, part in enumerate(sums[1:], 1):
            own = own + moved(part, dz * inner, pairs).astype(jnp.float32)
        return own.astype(jnp.bfloat16)

    def outer_columns(own, among, halves, after=()):
        pairs = [(a, a) for a in among]
        powers = [1 << p for p in range(outer.bit_length() - 1)]
        near = {0: own, **{dz: moved(own, dz * inner, pairs) for dz in reversed(powers)}}
        got = along_outer(near, pairs, after)
        return [jnp.stack([got[dz] for dz in some]) for some in halves]

    def all_columns(columns, among):
        pairs = [(a, a) for a in among]
        return [[c] + [moved(c, dx, pairs) for dx in range(1, inner)] for c in columns]

    upper = list(range(sections - 1, half - 1, -1))
    lower = list(range(half - 1, -1, -1))
    rot_outs = [None] * sections

    first = lower + upper[1:]
    own, others, arrived = rotate_begin(inputs, first)
    near, side = spread(top, [(upper[0], upper[0])])
    weights = resident(at, weights)
    halves = [order]
    sums = added(at, lower, own, arrived)
    low = summed(sums, lower)
    sent, before, within = ({0: top, **near}, side), others, sums
    for turn in upper:
        grad, blocks = relay(turn, sent, before, within, weights)
        if turn != upper[-1]:
            sent = handed_down(grad, turn - 1)
            rot_outs[turn] = rotated(turn, blocks)
            before, within = [low], [rot_outs[turn]]
        if turn == upper[0]:
            inputs, _ = lax.optimization_barrier((inputs, grad))
            last_own, last_others, last_arrived = rotate_begin(inputs, upper[:1])
            before, within = before + last_others, within + last_arrived
    low = outer_columns(low, lower, halves, [grad])
    sent = handed_down(grad, lower[0], low)
    if len(lower) == 1:
        low = all_columns(low, lower)
    rot_outs[upper[-1]] = rotated(upper[-1], blocks)
    last_cols = resident(at, out_cols, 0)
    own, last_own, _ = lax.optimization_barrier((own, last_own, sent[0][0]))
    before, within = [], [rot_outs[upper[-1]]]
    for turn in lower:
        grad, blocks = relay(turn, sent, before, within, weights if turn else last_cols)
        if turn != 0:
            sent = handed_down(grad, turn - 1)
            rot_outs[turn] = rotated(turn, blocks)
            before, within = [], [rot_outs[turn]]
        if turn == lower[0] and turn != 0:
            low, _ = lax.optimization_barrier((low, sent[0][0]))
            low = all_columns(low, lower)
            within = within + jax.tree.leaves(low)
    rot_outs[0] = grad
    sums = added(at, upper[:1], last_own, last_arrived, added(at, upper[1:], own, arrived))
    high = all_columns(outer_columns(summed(sums, upper), upper, [order]), upper)

    def runs(parts):
        place = {dz: (a, i) for a, some in enumerate(parts) for i, dz in enumerate(some)}
        return [(place[p // inner][0] * inner + p % inner, place[p // inner][1]) for p in range(shards)]

    low, high = jax.tree.leaves(low), jax.tree.leaves(high)
    return mean_square(
        at, half, rot_outs, low, high, runs(halves), runs([order]), micro, seq
    )[None]


def solution(mesh):
    return jax.shard_map(
        per_device,
        mesh=mesh,
        in_specs=(
            P("section", None, None, "shard"),
            P(None, None, "shard"),
            P("section", None, "shard"),
            P("section", None, "shard"),
            P("section", "shard", None),
        ),
        out_specs=P("section", "shard", None),
        check_vma=False,
    )
```

```python
import jax
import jax.numpy as jnp
from jax import lax
from jax.experimental import pallas as pl
from jax.experimental.pallas import tpu as pltpu
from jax.sharding import PartitionSpec as P

VMEM = pl.BlockSpec(memory_space=pltpu.VMEM)
SMEM = pl.BlockSpec(memory_space=pltpu.SMEM)
HBM = pl.BlockSpec(memory_space=pltpu.HBM)


def params(megabytes):
    return pltpu.CompilerParams(vmem_limit_bytes=megabytes * 1024 * 1024)


def in_hbm(array):
    return pltpu.with_memory_space_constraint(array, pltpu.HBM)


def run_of(ref, axis, at, length):
    part = pl.ds(pl.multiple_of(at * length, length), length)
    return ref.at[part, :] if axis == 0 else ref.at[:, part]


def resident(at, weights, only=None):
    count = at.shape[0] - 1
    depth, cols = weights.shape[0] // count, weights.shape[1]

    def body(at, weights_ref, out_ref, sems):
        def copy(i):
            return pltpu.make_async_copy(
                run_of(weights_ref, 0, at[1 + i], depth), out_ref.at[i], sems.at[i]
            )

        @pl.when((at[0] == only) if only is not None else (at[0] >= 0))
        def _():
            for i in range(count):
                copy(i).start()
            for i in range(count):
                copy(i).wait()

    return pl.pallas_call(
        body,
        in_specs=[SMEM, HBM],
        out_specs=VMEM,
        out_shape=jax.ShapeDtypeStruct((count, depth, cols), weights.dtype),
        scratch_shapes=[pltpu.SemaphoreType.DMA((count,))],
        compiler_params=params(4),
        name="resident",
    )(at, in_hbm(weights))


def block_dot(at, turn, blocks, weights, parts, base, out_type):
    rows, depth = blocks[0].shape
    cols = weights.shape[2]
    width = 256 if cols % 256 == 0 else cols
    count = len(blocks)

    def body(at, weights_ref, *refs):
        @pl.when(at[0] == turn)
        def _():
            def tile(j, _):
                here = pl.ds(pl.multiple_of(j * width, width), width)
                total = None if base is None else refs[count][:, here].astype(jnp.float32)
                for block_ref, part in zip(refs[:count], parts):
                    product = jnp.dot(
                        block_ref[...],
                        weights_ref[part, :, here],
                        preferred_element_type=jnp.float32,
                    )
                    total = product if total is None else total + product
                refs[-1][:, here] = total.astype(out_type)
                return 0

            lax.fori_loop(0, cols // width, tile, 0)

    return pl.pallas_call(
        body,
        in_specs=[SMEM] + [VMEM] * (1 + count + (base is not None)),
        out_specs=VMEM,
        out_shape=jax.ShapeDtypeStruct((rows, cols), out_type),
        compiler_params=params(4),
        name="block_dot",
    )(at, weights, *blocks, *([] if base is None else [base]))


def stream_dot(at, turn, blocks, weights, parts, out_type):
    rows, depth = blocks[0].shape
    cols = weights.shape[1]
    count = len(blocks)

    def body(at, weights_ref, *refs):
        block_refs, (out_ref, runs, sems) = refs[:count], refs[-3:]

        def copy(k):
            return pltpu.make_async_copy(
                run_of(weights_ref, 0, at[1 + parts[k]], depth), runs.at[k], sems.at[k]
            )

        @pl.when(at[0] == turn)
        def _():
            for k in range(count):
                copy(k).start()
            total = None
            for k in range(count):
                copy(k).wait()
                part = jnp.dot(block_refs[k][...], runs[k], preferred_element_type=jnp.float32)
                total = part if total is None else total + part
            out_ref[...] = total.astype(out_type)

    return pl.pallas_call(
        body,
        in_specs=[SMEM, HBM] + [VMEM] * count,
        out_specs=VMEM,
        out_shape=jax.ShapeDtypeStruct((rows, cols), out_type),
        scratch_shapes=[
            pltpu.VMEM((count, depth, cols), weights.dtype),
            pltpu.SemaphoreType.DMA((count,)),
        ],
        compiler_params=params(14),
        name="stream_dot",
    )(at, in_hbm(weights), *blocks)


def partials(at, among, inputs, weights, inner):
    rows, depth = inputs.shape
    count = at.shape[0] - 1
    width = weights.shape[1] // count

    def body(at, weights_ref, inputs_ref, *refs):
        out_refs, (runs, sems) = refs[:inner], refs[inner:]
        order = [n for dx in [*range(1, inner), 0] for n in range(dx, count, inner)]

        def copy(n):
            return pltpu.make_async_copy(
                run_of(weights_ref, 1, at[1 + n], width), runs.at[n], sems.at[n]
            )

        @pl.when((at[0] >= min(among)) & (at[0] <= max(among)))
        def _():
            for n in order:
                copy(n).start()
            for n in order:
                copy(n).wait()
                total = jnp.dot(inputs_ref[...], runs[n], preferred_element_type=jnp.float32)
                out_ref = out_refs[n % inner]
                out_ref[n // inner] = total.astype(out_ref.dtype)

    return pl.pallas_call(
        body,
        in_specs=[SMEM, HBM, VMEM],
        out_specs=[VMEM] * inner,
        out_shape=[
            jax.ShapeDtypeStruct((count // inner, rows, width), jnp.bfloat16 if dx else jnp.float32)
            for dx in range(inner)
        ],
        scratch_shapes=[
            pltpu.VMEM((count, depth, width), weights.dtype),
            pltpu.SemaphoreType.DMA((count,)),
        ],
        compiler_params=params(14),
        name="partials",
    )(at, in_hbm(weights), inputs)


def added(at, among, own, arrived, old=()):
    count, rows, width = own.shape

    def body(at, own_ref, *refs):
        arrived_refs, out_refs = refs[: len(arrived)], refs[len(arrived) + len(old) :]

        @pl.when((at[0] >= min(among)) & (at[0] <= max(among)))
        def _():
            for n in range(count):
                total = own_ref[n]
                for ref in arrived_refs:
                    total = total + ref[n].astype(jnp.float32)
                out_refs[n][...] = total.astype(out_refs[n].dtype)

    return pl.pallas_call(
        body,
        in_specs=[SMEM] + [VMEM] * (1 + len(arrived) + len(old)),
        input_output_aliases={2 + len(arrived) + n: n for n in range(len(old))},
        out_specs=[VMEM] * count,
        out_shape=[
            jax.ShapeDtypeStruct((rows, width), jnp.bfloat16 if n else jnp.float32)
            for n in range(count)
        ],
        compiler_params=params(4),
        name="added",
    )(at, own, *arrived, *old)


def mean_square(at, half, rot_outs, low, high, low_runs, high_runs, micro, seq):
    _, rows, width = low[0].shape
    eig_rows = rot_outs[0].shape[1]
    count, sections = len(low_runs), len(rot_outs)

    def body(at, *refs):
        rot_refs, refs = refs[:sections], refs[sections:]
        low_refs, refs = refs[: len(low)], refs[len(low) :]
        high_refs, refs = refs[: len(high)], refs[len(high) :]
        eig_ref, rot, block, result, sems = refs
        for s in range(sections):

            @pl.when(at[0] == s)
            def _():
                rot[...] = rot_refs[s][...]

        def copy(n):
            return pltpu.make_async_copy(
                result.at[n % 2], run_of(eig_ref, 1, at[1 + n], width), sems.at[n % 2]
            )

        for n in range(count):

            @pl.when(at[0] >= half)
            def _():
                a, i = high_runs[n]
                block[...] = high_refs[a][i]

            @pl.when(at[0] < half)
            def _():
                a, i = low_runs[n]
                block[...] = low_refs[a][i]

            if n >= 2:
                copy(n - 2).wait()
            for m in range(micro):
                rows_of = slice(m * seq, (m + 1) * seq)
                product = lax.dot_general(
                    rot[rows_of, :],
                    block[rows_of, :],
                    (((0,), (0,)), ((), ())),
                    preferred_element_type=jnp.float32,
                )
                square = product * product
                total = square if m == 0 else result[n % 2] + square
                result[n % 2] = total if m < micro - 1 else total * (1.0 / (seq * micro))
            copy(n).start()
        for n in range(max(0, count - 2), count):
            copy(n).wait()

    return pl.pallas_call(
        body,
        in_specs=[SMEM] + [VMEM] * (sections + len(low) + len(high)),
        out_specs=HBM,
        out_shape=jax.ShapeDtypeStruct((eig_rows, count * width), jnp.float32),
        scratch_shapes=[
            pltpu.VMEM((rows, eig_rows), rot_outs[0].dtype),
            pltpu.VMEM((rows, width), rot_outs[0].dtype),
            pltpu.VMEM((2, eig_rows, width), jnp.float32),
            pltpu.SemaphoreType.DMA((2,)),
        ],
        compiler_params=params(14),
        name="mean_square",
    )(at, *rot_outs, *low, *high)


def per_device(activations, top_grad, projection, basis_out, basis_in):
    sections = lax.axis_size("section")
    shards = lax.axis_size("shard")
    micro, seq, feat_loc = top_grad.shape
    rows = micro * seq
    inputs = activations[0].reshape(rows, feat_loc)
    top = top_grad.reshape(rows, feat_loc)
    weights, out_cols = projection[0], basis_out[0]
    half = sections // 2

    inner = 1
    while 2 * (2 * inner) ** 2 <= shards:
        inner *= 2
    outer = shards // inner
    shard = lax.axis_index("shard")
    at = jnp.stack(
        [jnp.int32(lax.axis_index("section"))] + [jnp.int32(shard ^ p) for p in range(shards)]
    )

    def moved(block, flip, pairs):
        route = [(a * shards + i, b * shards + (i ^ flip)) for a, b in pairs for i in range(shards)]
        return lax.ppermute(block, ("section", "shard"), route)

    def spread(block, pairs):
        powers = [1 << p for p in range(outer.bit_length() - 1)]
        near = {dz: moved(block, dz * inner, pairs) for dz in reversed(powers)}
        return near, {dx: moved(block, dx, pairs) for dx in range(1, inner)}

    def along_outer(near, pairs, after=()):
        got = dict(near)
        for dz in range(outer):
            low = dz & -dz
            if dz not in got:
                block, *_ = lax.optimization_barrier((got[dz ^ low], *after))
                got[dz] = moved(block, low * inner, pairs)
        return got

    def handed_down(grad, turn, after=()):
        own = moved(grad, 0, [(turn + 1, turn)])
        if turn % 2 == 0:
            near, side = spread(grad, [(turn + 1, turn)])
        else:
            own, *_ = lax.optimization_barrier((own, *after))
            near, side = spread(own, [(turn, turn)])
        return {0: own, **near}, side

    order = [0] + [1 << p for p in reversed(range(outer.bit_length() - 1))]
    order += [dz for dz in range(outer) if dz not in order]

    def relay(turn, sent, before, within, matrix):
        near, side = sent
        got = along_outer(near, [(turn, turn)])
        start, *_ = lax.optimization_barrier((near[0], *before))

        def products(dots, base, last):
            blocks, parts = [block for block, _ in dots], [part for _, part in dots]
            out_type = jnp.bfloat16 if last else jnp.float32
            return block_dot(at, turn, blocks, matrix, parts, base, out_type)

        blocks = {(0, 0): start, **{(0, dx): block for dx, block in side.items()}}
        dots = [(block, dx) for (_, dx), block in blocks.items()]
        totals = [products(dots, None if turn == 0 else start, outer == 1)]
        for n in range(1, outer + 1):
            if n < outer:
                dz = order[n]
                ties = [totals[0] if n > 1 or turn < sections - 1 else matrix]
                ties += [blocks[order[max(0, n - 2)], dx] for dx in range(1, inner)]
                block, *_ = lax.optimization_barrier(
                    (got[dz], *ties, *(within if n == outer - 1 else []))
                )
                blocks[dz, 0] = got[dz]
                for dx in range(1, inner):
                    blocks[dz, dx] = moved(block, dx, [(turn, turn)])
            if n > 1:
                dz = order[n - 1]
                dots = [(blocks[dz, dx], dz * inner + dx) for dx in range(inner)]
                if n == outer - 1:
                    dots.append((blocks[order[n], 0], order[n] * inner))
                if n == outer and outer > 2 and inner > 1:
                    dots = dots[1:]
                totals.append(products(dots, totals[-1], n == outer))
        return totals[-1], blocks

    def rotated(turn, blocks):
        parts = [dz * inner + dx for dz, dx in blocks]
        return stream_dot(at, turn, list(blocks.values()), out_cols, parts, jnp.bfloat16)

    def rotate_begin(inputs, among):
        pairs = [(a, a) for a in among]
        own, *others = partials(at, among, inputs, basis_in[0], inner)
        return own, others, [moved(other, 1 + n, pairs) for n, other in enumerate(others)]

    def summed(sums, among):
        pairs = [(a, a) for a in among]
        own = sums[0]
        for dz, part in enumerate(sums[1:], 1):
            own = own + moved(part, dz * inner, pairs).astype(jnp.float32)
        return own.astype(jnp.bfloat16)

    def outer_columns(own, among, halves, after=()):
        pairs = [(a, a) for a in among]
        powers = [1 << p for p in range(outer.bit_length() - 1)]
        near = {0: own, **{dz: moved(own, dz * inner, pairs) for dz in reversed(powers)}}
        got = along_outer(near, pairs, after)
        return [jnp.stack([got[dz] for dz in some]) for some in halves]

    def all_columns(columns, among):
        pairs = [(a, a) for a in among]
        all_parts = []
        for column in columns:
            tied, *_ = lax.optimization_barrier((column, *(all_parts[-1][1:] if all_parts else [])))
            all_parts.append([column] + [moved(tied, dx, pairs) for dx in range(1, inner)])
        return all_parts

    upper = list(range(sections - 1, half - 1, -1))
    lower = list(range(half - 1, -1, -1))
    rot_outs = [None] * sections

    first = lower + upper[1:]
    own, others, arrived = rotate_begin(inputs, first)
    near, side = spread(top, [(upper[0], upper[0])])
    weights = resident(at, weights)
    halves = [order[: outer // 2], order[outer // 2 :]] if outer > 1 else [order]
    sums = added(at, lower, own, arrived)
    low = summed(sums, lower)
    sent, before, within = ({0: top, **near}, side), others, sums
    for turn in upper:
        grad, blocks = relay(turn, sent, before, within, weights)
        if turn != upper[-1]:
            sent = handed_down(grad, turn - 1)
            rot_outs[turn] = rotated(turn, blocks)
            before, within = [low], [rot_outs[turn]]
        if turn == upper[0]:
            inputs, _ = lax.optimization_barrier((inputs, grad))
            last_own, last_others, last_arrived = rotate_begin(inputs, upper[:1])
            before, within = before + last_others, within + last_arrived
    low = outer_columns(low, lower, halves, [grad])
    columns, low = low, all_columns(low, lower)
    sent = handed_down(grad, lower[0], columns + low[0][1:])
    rot_outs[upper[-1]] = rotated(upper[-1], blocks)
    last_cols = resident(at, out_cols, 0)
    own, last_own, _ = lax.optimization_barrier((own, last_own, sent[0][0]))
    before, within = [], [rot_outs[upper[-1]], *low[-1][1:]]
    for turn in lower:
        grad, blocks = relay(turn, sent, before, within, weights if turn else last_cols)
        if turn != 0:
            sent = handed_down(grad, turn - 1)
            rot_outs[turn] = rotated(turn, blocks)
            before, within = [], [rot_outs[turn]]
    rot_outs[0] = grad
    sums = added(at, upper[:1], last_own, last_arrived, added(at, upper[1:], own, arrived))
    high = all_columns(outer_columns(summed(sums, upper), upper, [order]), upper)

    def runs(parts):
        place = {dz: (a, i) for a, some in enumerate(parts) for i, dz in enumerate(some)}
        return [(place[p // inner][0] * inner + p % inner, place[p // inner][1]) for p in range(shards)]

    low, high = jax.tree.leaves(low), jax.tree.leaves(high)
    return mean_square(
        at, half, rot_outs, low, high, runs(halves), runs([order]), micro, seq
    )[None]


def solution(mesh):
    return jax.shard_map(
        per_device,
        mesh=mesh,
        in_specs=(
            P("section", None, None, "shard"),
            P(None, None, "shard"),
            P("section", None, "shard"),
            P("section", None, "shard"),
            P("section", "shard", None),
        ),
        out_specs=P("section", "shard", None),
        check_vma=False,
    )
```

```python
import jax
import jax.numpy as jnp
from jax import lax
from jax.experimental import pallas as pl
from jax.experimental.pallas import tpu as pltpu
from jax.sharding import PartitionSpec as P

VMEM = pl.BlockSpec(memory_space=pltpu.VMEM)
SMEM = pl.BlockSpec(memory_space=pltpu.SMEM)
HBM = pl.BlockSpec(memory_space=pltpu.HBM)


def params(megabytes):
    return pltpu.CompilerParams(vmem_limit_bytes=megabytes * 1024 * 1024)


def in_hbm(array):
    return pltpu.with_memory_space_constraint(array, pltpu.HBM)


def run_of(ref, axis, at, length):
    part = pl.ds(pl.multiple_of(at * length, length), length)
    return ref.at[part, :] if axis == 0 else ref.at[:, part]


def resident(at, weights, only=None):
    count = at.shape[0] - 1
    depth, cols = weights.shape[0] // count, weights.shape[1]

    def body(at, weights_ref, out_ref, sems):
        def copy(i):
            return pltpu.make_async_copy(
                run_of(weights_ref, 0, at[1 + i], depth), out_ref.at[i], sems.at[i]
            )

        @pl.when((at[0] == only) if only is not None else (at[0] >= 0))
        def _():
            for i in range(count):
                copy(i).start()
            for i in range(count):
                copy(i).wait()

    return pl.pallas_call(
        body,
        in_specs=[SMEM, HBM],
        out_specs=VMEM,
        out_shape=jax.ShapeDtypeStruct((count, depth, cols), weights.dtype),
        scratch_shapes=[pltpu.SemaphoreType.DMA((count,))],
        compiler_params=params(4),
        name="resident",
    )(at, in_hbm(weights))


def block_dot(at, turn, blocks, weights, parts, base, out_type):
    rows, depth = blocks[0].shape
    cols = weights.shape[2]
    width = 256 if cols % 256 == 0 else cols
    count = len(blocks)

    def body(at, weights_ref, *refs):
        @pl.when(at[0] == turn)
        def _():
            def tile(j, _):
                here = pl.ds(pl.multiple_of(j * width, width), width)
                total = None if base is None else refs[count][:, here].astype(jnp.float32)
                for block_ref, part in zip(refs[:count], parts):
                    product = jnp.dot(
                        block_ref[...],
                        weights_ref[part, :, here],
                        preferred_element_type=jnp.float32,
                    )
                    total = product if total is None else total + product
                refs[-1][:, here] = total.astype(out_type)
                return 0

            lax.fori_loop(0, cols // width, tile, 0)

    return pl.pallas_call(
        body,
        in_specs=[SMEM] + [VMEM] * (1 + count + (base is not None)),
        out_specs=VMEM,
        out_shape=jax.ShapeDtypeStruct((rows, cols), out_type),
        compiler_params=params(4),
        name="block_dot",
    )(at, weights, *blocks, *([] if base is None else [base]))


def stream_dot(at, turn, blocks, weights, parts, out_type):
    rows, depth = blocks[0].shape
    cols = weights.shape[1]
    count = len(blocks)

    def body(at, weights_ref, *refs):
        block_refs, (out_ref, runs, sems) = refs[:count], refs[-3:]

        def copy(k):
            return pltpu.make_async_copy(
                run_of(weights_ref, 0, at[1 + parts[k]], depth), runs.at[k], sems.at[k]
            )

        @pl.when(at[0] == turn)
        def _():
            for k in range(count):
                copy(k).start()
            total = None
            for k in range(count):
                copy(k).wait()
                part = jnp.dot(block_refs[k][...], runs[k], preferred_element_type=jnp.float32)
                total = part if total is None else total + part
            out_ref[...] = total.astype(out_type)

    return pl.pallas_call(
        body,
        in_specs=[SMEM, HBM] + [VMEM] * count,
        out_specs=VMEM,
        out_shape=jax.ShapeDtypeStruct((rows, cols), out_type),
        scratch_shapes=[
            pltpu.VMEM((count, depth, cols), weights.dtype),
            pltpu.SemaphoreType.DMA((count,)),
        ],
        compiler_params=params(14),
        name="stream_dot",
    )(at, in_hbm(weights), *blocks)


def partials(at, among, inputs, weights, inner):
    rows, depth = inputs.shape
    count = at.shape[0] - 1
    width = weights.shape[1] // count

    def body(at, weights_ref, inputs_ref, *refs):
        out_refs, (runs, sems) = refs[:inner], refs[inner:]
        order = [n for dx in [*range(1, inner), 0] for n in range(dx, count, inner)]

        def copy(n):
            return pltpu.make_async_copy(
                run_of(weights_ref, 1, at[1 + n], width), runs.at[n], sems.at[n]
            )

        @pl.when((at[0] >= min(among)) & (at[0] <= max(among)))
        def _():
            for n in order:
                copy(n).start()
            for n in order:
                copy(n).wait()
                total = jnp.dot(inputs_ref[...], runs[n], preferred_element_type=jnp.float32)
                out_ref = out_refs[n % inner]
                out_ref[n // inner] = total.astype(out_ref.dtype)

    return pl.pallas_call(
        body,
        in_specs=[SMEM, HBM, VMEM],
        out_specs=[VMEM] * inner,
        out_shape=[
            jax.ShapeDtypeStruct((count // inner, rows, width), jnp.bfloat16 if dx else jnp.float32)
            for dx in range(inner)
        ],
        scratch_shapes=[
            pltpu.VMEM((count, depth, width), weights.dtype),
            pltpu.SemaphoreType.DMA((count,)),
        ],
        compiler_params=params(14),
        name="partials",
    )(at, in_hbm(weights), inputs)


def added(at, among, own, arrived, old=()):
    count, rows, width = own.shape

    def body(at, own_ref, *refs):
        arrived_refs, out_refs = refs[: len(arrived)], refs[len(arrived) + len(old) :]

        @pl.when((at[0] >= min(among)) & (at[0] <= max(among)))
        def _():
            for n in range(count):
                total = own_ref[n]
                for ref in arrived_refs:
                    total = total + ref[n].astype(jnp.float32)
                out_refs[n][...] = total.astype(out_refs[n].dtype)

    return pl.pallas_call(
        body,
        in_specs=[SMEM] + [VMEM] * (1 + len(arrived) + len(old)),
        input_output_aliases={2 + len(arrived) + n: n for n in range(len(old))},
        out_specs=[VMEM] * count,
        out_shape=[
            jax.ShapeDtypeStruct((rows, width), jnp.bfloat16 if n else jnp.float32)
            for n in range(count)
        ],
        compiler_params=params(4),
        name="added",
    )(at, own, *arrived, *old)


def mean_square(at, half, rot_outs, low, high, low_runs, high_runs, micro, seq):
    _, rows, width = low[0].shape
    eig_rows = rot_outs[0].shape[1]
    count, sections = len(low_runs), len(rot_outs)

    def body(at, *refs):
        rot_refs, refs = refs[:sections], refs[sections:]
        low_refs, refs = refs[: len(low)], refs[len(low) :]
        high_refs, refs = refs[: len(high)], refs[len(high) :]
        eig_ref, rot, block, result, sems = refs
        for s in range(sections):

            @pl.when(at[0] == s)
            def _():
                rot[...] = rot_refs[s][...]

        def copy(n):
            return pltpu.make_async_copy(
                result.at[n % 2], run_of(eig_ref, 1, at[1 + n], width), sems.at[n % 2]
            )

        for n in range(count):

            @pl.when(at[0] >= half)
            def _():
                a, i = high_runs[n]
                block[...] = high_refs[a][i]

            @pl.when(at[0] < half)
            def _():
                a, i = low_runs[n]
                block[...] = low_refs[a][i]

            if n >= 2:
                copy(n - 2).wait()
            for m in range(micro):
                rows_of = slice(m * seq, (m + 1) * seq)
                product = lax.dot_general(
                    rot[rows_of, :],
                    block[rows_of, :],
                    (((0,), (0,)), ((), ())),
                    preferred_element_type=jnp.float32,
                )
                square = product * product
                total = square if m == 0 else result[n % 2] + square
                result[n % 2] = total if m < micro - 1 else total * (1.0 / (seq * micro))
            copy(n).start()
        for n in range(max(0, count - 2), count):
            copy(n).wait()

    return pl.pallas_call(
        body,
        in_specs=[SMEM] + [VMEM] * (sections + len(low) + len(high)),
        out_specs=HBM,
        out_shape=jax.ShapeDtypeStruct((eig_rows, count * width), jnp.float32),
        scratch_shapes=[
            pltpu.VMEM((rows, eig_rows), rot_outs[0].dtype),
            pltpu.VMEM((rows, width), rot_outs[0].dtype),
            pltpu.VMEM((2, eig_rows, width), jnp.float32),
            pltpu.SemaphoreType.DMA((2,)),
        ],
        compiler_params=params(14),
        name="mean_square",
    )(at, *rot_outs, *low, *high)


def per_device(activations, top_grad, projection, basis_out, basis_in):
    sections = lax.axis_size("section")
    shards = lax.axis_size("shard")
    micro, seq, feat_loc = top_grad.shape
    rows = micro * seq
    inputs = activations[0].reshape(rows, feat_loc)
    top = top_grad.reshape(rows, feat_loc)
    weights, out_cols = projection[0], basis_out[0]
    half = sections // 2

    inner = 1
    while 2 * (2 * inner) ** 2 <= shards:
        inner *= 2
    outer = shards // inner
    shard = lax.axis_index("shard")
    at = jnp.stack(
        [jnp.int32(lax.axis_index("section"))] + [jnp.int32(shard ^ p) for p in range(shards)]
    )

    def moved(block, flip, pairs):
        route = [(a * shards + i, b * shards + (i ^ flip)) for a, b in pairs for i in range(shards)]
        return lax.ppermute(block, ("section", "shard"), route)

    def spread(block, pairs):
        powers = [1 << p for p in range(outer.bit_length() - 1)]
        near = {dz: moved(block, dz * inner, pairs) for dz in reversed(powers)}
        return near, {dx: moved(block, dx, pairs) for dx in range(1, inner)}

    def along_outer(near, pairs, after=()):
        got = dict(near)
        for dz in range(outer):
            low = dz & -dz
            if dz not in got:
                block, *_ = lax.optimization_barrier((got[dz ^ low], *after))
                got[dz] = moved(block, low * inner, pairs)
        return got

    def handed_down(grad, turn, after=()):
        own = moved(grad, 0, [(turn + 1, turn)])
        if turn % 2 == 0:
            near, side = spread(grad, [(turn + 1, turn)])
        else:
            own, *_ = lax.optimization_barrier((own, *after))
            near, side = spread(own, [(turn, turn)])
        return {0: own, **near}, side

    order = [0] + [1 << p for p in reversed(range(outer.bit_length() - 1))]
    order += [dz for dz in range(outer) if dz not in order]

    def relay(turn, sent, before, within, matrix):
        near, side = sent
        got = along_outer(near, [(turn, turn)])
        start, *_ = lax.optimization_barrier((near[0], *before))

        def products(dots, base, last):
            blocks, parts = [block for block, _ in dots], [part for _, part in dots]
            out_type = jnp.bfloat16 if last else jnp.float32
            return block_dot(at, turn, blocks, matrix, parts, base, out_type)

        blocks = {(0, 0): start, **{(0, dx): block for dx, block in side.items()}}
        dots = [(block, dx) for (_, dx), block in blocks.items()]
        totals = [products(dots, None if turn == 0 else start, outer == 1)]
        for n in range(1, outer + 1):
            if n < outer:
                dz = order[n]
                ties = [totals[0] if n > 1 or turn < sections - 1 else matrix]
                ties += [blocks[order[max(0, n - 2)], dx] for dx in range(1, inner)]
                block, *_ = lax.optimization_barrier(
                    (got[dz], *ties, *(within if n == outer - 1 else []))
                )
                blocks[dz, 0] = got[dz]
                for dx in range(1, inner):
                    blocks[dz, dx] = moved(block, dx, [(turn, turn)])
            if n > 1:
                dz = order[n - 1]
                dots = [(blocks[dz, dx], dz * inner + dx) for dx in range(inner)]
                if n == outer - 1:
                    dots.append((blocks[order[n], 0], order[n] * inner))
                if n == outer and outer > 2 and inner > 1:
                    dots = dots[1:]
                totals.append(products(dots, totals[-1], n == outer))
        return totals[-1], blocks

    def rotated(turn, blocks):
        parts = [dz * inner + dx for dz, dx in blocks]
        return stream_dot(at, turn, list(blocks.values()), out_cols, parts, jnp.bfloat16)

    def rotate_begin(inputs, among):
        pairs = [(a, a) for a in among]
        own, *others = partials(at, among, inputs, basis_in[0], inner)
        return own, others, [moved(other, 1 + n, pairs) for n, other in enumerate(others)]

    def summed(sums, among):
        pairs = [(a, a) for a in among]
        own = sums[0]
        for dz, part in enumerate(sums[1:], 1):
            own = own + moved(part, dz * inner, pairs).astype(jnp.float32)
        return own.astype(jnp.bfloat16)

    def outer_columns(own, among, halves, after=()):
        pairs = [(a, a) for a in among]
        powers = [1 << p for p in range(outer.bit_length() - 1)]
        near = {0: own, **{dz: moved(own, dz * inner, pairs) for dz in reversed(powers)}}
        got = along_outer(near, pairs, after)
        return [jnp.stack([got[dz] for dz in some]) for some in halves]

    def all_columns(columns, among):
        pairs = [(a, a) for a in among]
        all_parts = []
        for column in columns:
            tied, *_ = lax.optimization_barrier((column, *(all_parts[-1][1:] if all_parts else [])))
            all_parts.append([column] + [moved(tied, dx, pairs) for dx in range(1, inner)])
        return all_parts

    upper = list(range(sections - 1, half - 1, -1))
    lower = list(range(half - 1, -1, -1))
    rot_outs = [None] * sections

    first = lower + upper[1:]
    own, others, arrived = rotate_begin(inputs, first)
    near, side = spread(top, [(upper[0], upper[0])])
    weights = resident(at, weights)
    halves = [[0, 1], [dz for dz in order if dz > 1]] if outer > 2 else [order]
    sums = added(at, lower, own, arrived)
    low = summed(sums, lower)
    sent, before, within = ({0: top, **near}, side), others, sums
    for turn in upper:
        grad, blocks = relay(turn, sent, before, within, weights)
        if turn != upper[-1]:
            sent = handed_down(grad, turn - 1)
            rot_outs[turn] = rotated(turn, blocks)
            before, within = [low], [rot_outs[turn]]
        if turn == upper[0]:
            inputs, _ = lax.optimization_barrier((inputs, grad))
            last_own, last_others, last_arrived = rotate_begin(inputs, upper[:1])
            before, within = before + last_others, within + last_arrived
    low = outer_columns(low, lower, halves, [grad])
    columns, low = low, all_columns(low, lower)
    sent = handed_down(grad, lower[0], columns + low[0][1:])
    rot_outs[upper[-1]] = rotated(upper[-1], blocks)
    last_cols = resident(at, out_cols, 0)
    own, last_own, _ = lax.optimization_barrier((own, last_own, sent[0][0]))
    before, within = [], [rot_outs[upper[-1]], *low[-1][1:]]
    for turn in lower:
        grad, blocks = relay(turn, sent, before, within, weights if turn else last_cols)
        if turn != 0:
            sent = handed_down(grad, turn - 1)
            rot_outs[turn] = rotated(turn, blocks)
            before, within = [], [rot_outs[turn]]
    rot_outs[0] = grad
    sums = added(at, upper[:1], last_own, last_arrived, added(at, upper[1:], own, arrived))
    high = all_columns(outer_columns(summed(sums, upper), upper, [order]), upper)

    def runs(parts):
        place = {dz: (a, i) for a, some in enumerate(parts) for i, dz in enumerate(some)}
        return [(place[p // inner][0] * inner + p % inner, place[p // inner][1]) for p in range(shards)]

    low, high = jax.tree.leaves(low), jax.tree.leaves(high)
    return mean_square(
        at, half, rot_outs, low, high, runs(halves), runs([order]), micro, seq
    )[None]


def solution(mesh):
    return jax.shard_map(
        per_device,
        mesh=mesh,
        in_specs=(
            P("section", None, None, "shard"),
            P(None, None, "shard"),
            P("section", None, "shard"),
            P("section", None, "shard"),
            P("section", "shard", None),
        ),
        out_specs=P("section", "shard", None),
        check_vma=False,
    )
```
